128 devices in a mesh: row: 8 (over x_lo, y), col: 16 (over x_hi, z, core).
Axes of the slice: x: 4 (x_hi: 2, x_lo: 2; x = x_hi * 2 + x_lo), y: 4, z: 4, core: 2. Of those that a mesh axis runs over, the one named last changes fastest.
Arguments:
- features: bfloat16 [131072, 128], P(('row', 'col')), may hold values from -6 to 6
- weight: bfloat16 [128, 128], replicated, may hold values from -0.5 to 0.5
- cotangent: bfloat16 [131072, 128], P(('row', 'col')), may hold values from -6 to 6
- degree: int32 [131072], P(('row', 'col')), may hold values from 1 to 64
- tile_vals: bfloat16 [8192, 128, 128], P(('row', 'col')), may hold values from -0.25 to 0.25
- tile_rows: int32 [8192], P(('row', 'col')), may hold values from 0 to 7
- tile_cols: int32 [8192], P(('row', 'col')), may hold values from 0 to 7
- tile_live: int32 [8192], P(('row', 'col')), may hold values 0 or 1
- send_index: int32 [1024, 4], P(('row', 'col')), may hold values from 0 to 7
- remote_vals: bfloat16 [4096, 128, 128], P(('row', 'col')), may hold values from -0.5 to 0.5
- remote_rows: int32 [1024, 4], P(('row', 'col')), may hold values from 0 to 7
- remote_live: int32 [1024, 4], P(('row', 'col')), may hold values 0 or 1
Outputs:
- out_z: bfloat16 [131072, 128], P(('row', 'col'))
- grad_x: bfloat16 [131072, 128], P(('row', 'col'))
- grad_w: float32 [128, 128], replicated
The draws below stay inside these ranges and needn't reach their ends.
Inputs may be any that keep to these rules, and one draw needn't show every extreme that they name: `tile_rows`: tile indices among one device's 1024 // 128 tiles.
All inputs are finite; a program needn't handle non-finite values. No bound on the sum of `tile_live` or of `remote_live` on one device may be relied on, other than what follows from the above.
Results may differ from the reference program's by a relative error of at most 0.0055.
Values may be sent and summed in bfloat16 or wider, within the bound.
A program may use at most 128 MiB of HBM per device.

```python
import jax
import jax.numpy as jnp
from jax import lax

FEAT = 128
FOUT = 128
TILE = 128
NODE_DEV = 1024
PER_PIECE = 4
SLOTS = 4
NODES = 131072
N_ROW = 8
N_COL = 16
DEVICES = 128


def place_ends(drawn, own_key, low, high):
    longest = drawn.shape.index(max(drawn.shape))
    spots = []
    for shift in (0, 1):
        where = [jax.random.randint(jax.random.fold_in(own_key, axis), (), 0, length) for axis, length in enumerate(drawn.shape)]
        where[longest] = (where[longest] + shift) % drawn.shape[longest]
        spots.append(tuple(where))
    return drawn.at[spots[0]].set(low).at[spots[1]].set(high)


def block_levels(stream_key, shape, pieces, smallest, top_value):
    level, own = 1.0, jax.random.fold_in(stream_key, 6)
    for axis_at, shards_of in pieces:
        heights = jnp.exp(jax.random.uniform(jax.random.fold_in(own, axis_at), (shards_of,), jnp.float32, smallest / len(pieces), top_value / len(pieces)))
        level = level * jnp.repeat(heights, shape[axis_at] // shards_of).reshape([-1 if axis == axis_at else 1 for axis in range(len(shape))])
    return level


def gaussian(rng, shape, scale, limit, cuts=(), kind=jnp.bfloat16):
    array = scale * jax.random.normal(rng, shape, jnp.float32)
    if cuts:
        array = array * block_levels(rng, shape, cuts, -0.22, 0.18)
    return jnp.clip(array, -limit, limit).astype(kind)


def setup_inputs(seed: int = 0) -> dict:
    key_of = jax.random.split(jax.random.key(seed), 13)
    features = gaussian(key_of[0], (NODES, FEAT), 1.0, 6.0, ((0, 128),))
    weight = gaussian(key_of[1], (FEAT, FOUT), FEAT ** -0.5, 0.5)
    cotangent = gaussian(key_of[2], (NODES, FOUT), 1.0, 6.0, ((0, 128),))
    degree = place_ends(jax.random.randint(key_of[3], (NODES,), 1, 65), jax.random.fold_in(key_of[3], 1), 1, 64).astype(jnp.int32)
    tile_vals = gaussian(key_of[4], (DEVICES * N_COL * PER_PIECE, TILE, TILE), (TILE * PER_PIECE) ** -0.5, 0.25, ((0, 128),))
    tile_rows = place_ends(jax.random.randint(key_of[5], (DEVICES * N_COL * PER_PIECE,), 0, NODE_DEV // TILE), jax.random.fold_in(key_of[5], 1), 0, (NODE_DEV // TILE) - 1).astype(jnp.int32)
    tile_cols = place_ends(jax.random.randint(key_of[6], (DEVICES * N_COL * PER_PIECE,), 0, NODE_DEV // TILE), jax.random.fold_in(key_of[6], 1), 0, (NODE_DEV // TILE) - 1).astype(jnp.int32)
    tile_live = place_ends((jax.random.randint(key_of[7], (DEVICES * N_COL * PER_PIECE,), 0, 4) < 3).astype(jnp.int32), jax.random.fold_in(key_of[7], 1), 0, 1)
    send_index = place_ends(jax.random.randint(key_of[8], (DEVICES * N_ROW, SLOTS), 0, NODE_DEV // TILE), jax.random.fold_in(key_of[8], 1), 0, (NODE_DEV // TILE) - 1).astype(jnp.int32)
    remote_vals = gaussian(key_of[9], (DEVICES * N_ROW * SLOTS, TILE, TILE), TILE ** -0.5, 0.5, ((0, 128),))
    remote_rows = place_ends(jax.random.randint(key_of[10], (DEVICES * N_ROW, SLOTS), 0, NODE_DEV // TILE), jax.random.fold_in(key_of[10], 1), 0, (NODE_DEV // TILE) - 1).astype(jnp.int32)
    remote_live = place_ends((jax.random.randint(key_of[11], (DEVICES * N_ROW, SLOTS), 0, 2) < 1).astype(jnp.int32), jax.random.fold_in(key_of[11], 1), 0, 1)
    return dict(features=features, weight=weight, cotangent=cotangent, degree=degree, tile_vals=tile_vals, tile_rows=tile_rows, tile_cols=tile_cols, tile_live=tile_live, send_index=send_index, remote_vals=remote_vals, remote_rows=remote_rows, remote_live=remote_live)


def reference(features, weight, cotangent, degree, tile_vals, tile_rows, tile_cols, tile_live, send_index, remote_vals, remote_rows, remote_live):
    highest = lax.Precision.HIGHEST
    tile_count = NODE_DEV // TILE
    inv_root = lax.rsqrt(degree.astype(jnp.float32))[:, None]
    scaled = (features.astype(jnp.float32) * inv_root).astype(jnp.bfloat16)
    scaled_grid = scaled.reshape(N_ROW, N_COL, tile_count, TILE, FEAT)
    dense_vals = tile_vals.reshape(N_ROW, N_COL, N_COL, PER_PIECE, TILE, TILE)
    dense_rows = tile_rows.reshape(N_ROW, N_COL, N_COL, PER_PIECE)
    dense_cols = tile_cols.reshape(N_ROW, N_COL, N_COL, PER_PIECE)
    dense_live = tile_live.reshape(N_ROW, N_COL, N_COL, PER_PIECE).astype(jnp.float32)
    sent_grid = send_index.reshape(N_ROW, N_COL, N_ROW, SLOTS).transpose(2, 1, 0, 3)
    remote_grid = remote_vals.reshape(N_ROW, N_COL, N_ROW, SLOTS, TILE, TILE)
    remote_at = remote_rows.reshape(N_ROW, N_COL, N_ROW, SLOTS)
    remote_on = remote_live.reshape(N_ROW, N_COL, N_ROW, SLOTS).astype(jnp.float32)
    own_piece = jnp.broadcast_to(jnp.arange(N_COL, dtype=jnp.int32)[:, None, None], (N_COL, N_COL, PER_PIECE))
    far_piece = jnp.broadcast_to(jnp.arange(N_COL, dtype=jnp.int32)[None, :, None], (N_COL, N_COL, PER_PIECE))
    col_index = jnp.broadcast_to(jnp.arange(N_COL, dtype=jnp.int32)[:, None, None], (N_COL, N_ROW, SLOTS))
    owner_index = jnp.broadcast_to(jnp.arange(N_ROW, dtype=jnp.int32)[None, :, None], (N_COL, N_ROW, SLOTS))
    empty_group = jnp.zeros((N_COL, tile_count, TILE, FEAT), jnp.float32)

    def dense_forward(inputs):
        grid, tiles_in, rows_in, cols_in, live_in = inputs
        picked = grid[far_piece, cols_in]
        product = jnp.einsum('abjik,abjkf->abjif', tiles_in.astype(jnp.float32), picked.astype(jnp.float32), precision=highest)
        product = product * live_in[..., None, None]
        return empty_group.at[own_piece, rows_in].add(product)

    def remote_forward(inputs):
        tiles_in, rows_in, live_in, sent = inputs
        picked = scaled_grid[owner_index, col_index, sent]
        product = jnp.einsum('crkij,crkjf->crkif', tiles_in.astype(jnp.float32), picked.astype(jnp.float32), precision=highest)
        product = product * live_in[..., None, None]
        return empty_group.at[col_index, rows_in].add(product)
    dense_sum = lax.map(dense_forward, (scaled_grid, dense_vals, dense_rows, dense_cols, dense_live))
    remote_sum = lax.map(remote_forward, (remote_grid, remote_at, remote_on, sent_grid))
    gathered = (dense_sum + remote_sum).reshape(NODES, FEAT)
    hidden = (inv_root * gathered).astype(jnp.bfloat16)
    out_z = jnp.dot(hidden, weight, preferred_element_type=jnp.float32).astype(jnp.bfloat16)
    grad_w = jnp.dot(hidden.T, cotangent, preferred_element_type=jnp.float32)
    pulled = (inv_root * jnp.dot(cotangent, weight.T, preferred_element_type=jnp.float32)).astype(jnp.bfloat16)
    pulled_grid = pulled.reshape(N_ROW, N_COL, tile_count, TILE, FEAT)

    def dense_backward(inputs):
        grid, tiles_in, rows_in, cols_in, live_in = inputs
        picked = grid[own_piece, rows_in]
        product = jnp.einsum('abjki,abjkf->abjif', tiles_in.astype(jnp.float32), picked.astype(jnp.float32), precision=highest)
        product = product * live_in[..., None, None]
        return empty_group.at[far_piece, cols_in].add(product)

    def remote_backward(running, inputs):
        grid, tiles_in, rows_in, live_in, sent = inputs
        picked = grid[col_index, rows_in]
        product = jnp.einsum('crkji,crkjf->crkif', tiles_in.astype(jnp.float32), picked.astype(jnp.float32), precision=highest)
        product = product * live_in[..., None, None]
        return (running.at[owner_index, col_index, sent].add(product), None)
    dense_grad = lax.map(dense_backward, (pulled_grid, dense_vals, dense_rows, dense_cols, dense_live))
    start_grad = jnp.zeros((N_ROW, N_COL, tile_count, TILE, FEAT), jnp.float32)
    remote_grad, unused = lax.scan(remote_backward, start_grad, (pulled_grid, remote_grid, remote_at, remote_on, sent_grid))
    spread = (dense_grad + remote_grad).reshape(NODES, FEAT)
    grad_x = (inv_root * spread).astype(jnp.bfloat16)
    return (out_z, grad_x, grad_w)
```

```python
import jax
import jax.numpy as jnp
from jax import lax
from jax.experimental import pallas as pl
from jax.experimental.pallas import tpu as pltpu
from jax.sharding import PartitionSpec as P

MESH = pl.DeviceIdType.MESH
BF16 = jnp.bfloat16
F32 = jnp.float32
TILE = 128
BLOCKS = 8
SLOTS = 4
HALF = 4
ROW_RELS = [(a, b) for a in range(2) for b in range(4)]
COL_RELS = [(a, b) for a in range(2) for b in range(4)]


def spot():
    row, col = lax.axis_index("row"), lax.axis_index("col")
    return row // 4, row % 4, col // 8, (col // 2) % 4, col % 2


def row_of(rel):
    x_lo, y, _, _, _ = spot()
    return ((x_lo + rel[0]) % 2) * 4 + (y + rel[1]) % 4


def col_of(rel, flip=0):
    _, _, x_hi, z, core = spot()
    return ((x_hi + rel[0]) % 2) * 8 + ((z + rel[1]) % 4) * 2 + (core + flip) % 2


def back_rel(rel):
    return (-rel[0]) % 2, (-rel[1]) % 4


def kernel(
    features,
    weight,
    cotangent,
    degree,
    tile_rows,
    tile_cols,
    tile_live,
    send_index,
    remote_rows,
    remote_live,
    tile_hbm,
    remote_hbm,
    out_z,
    grad_x,
    grad_w,
    tiles,
    remotes,
    inv_col,
    pulled,
    cot_t,
    prod,
    gathered,
    spread,
    outgoing,
    arrived,
    sent_back,
    returned,
    cross_out,
    cross_in,
    sums,
    ring_half,
    ring_full,
    pair_out,
    pair_in,
    wg,
    wg_core,
    wg_part,
    wg_col,
    wg_mine,
    wg_row,
    wg_half,
    wg_other,
    wg_all,
    send_sem,
    recv_sem,
    local_sem,
    *blocks,
):
    row, col = lax.axis_index("row"), lax.axis_index("col")
    _, _, x_hi, z, core = spot()
    copies = []

    def remote(src, dst, target):
        i = len(copies)
        copy = pltpu.make_async_remote_copy(
            src_ref=src,
            dst_ref=dst,
            send_sem=send_sem.at[i],
            recv_sem=recv_sem.at[i],
            device_id=target,
            device_id_type=MESH,
        )
        copies.append(copy)
        copy.start()
        return copy

    def to_row(rel):
        return (row_of(rel), col)

    def to_col(rel, flip=0):
        return (row, col_of(rel, flip))

    load_tiles = pltpu.make_async_copy(tile_hbm, tiles, local_sem.at[0])
    load_remotes = pltpu.make_async_copy(remote_hbm, remotes, local_sem.at[1])
    load_tiles.start()
    load_remotes.start()

    barrier = pltpu.get_barrier_semaphore()
    peers = [to_row(rel) for rel in ROW_RELS[1:]]
    peers += [to_col(rel) for rel in COL_RELS[1:]]
    peers += [to_col((0, 0), 1)]
    for peer in peers:
        pl.semaphore_signal(barrier, inc=1, device_id=peer, device_id_type=MESH)

    def block(rel, flip=0):
        return blocks[(rel[0] * 4 + rel[1] % 4) * 2 + flip]

    own = block((0, 0))
    inv_row = lax.rsqrt(degree[...].astype(F32))
    for b in range(BLOCKS):
        at = pl.ds(b * TILE, TILE)
        across = jnp.broadcast_to(inv_row[b : b + 1, :], (TILE, TILE)).T
        inv_col[at, :] = across
        own[b] = (features[at, :].astype(F32) * across).astype(BF16)

    pl.semaphore_wait(barrier, len(peers))

    def rows(ref, lo, hi):
        return ref.at[pl.ds(lo, hi - lo)]

    def push(rel_src, rel_dst, target, lo, hi):
        return remote(rows(block(rel_src), lo, hi), rows(block(rel_dst), lo, hi), target)

    z_up, z_down, x_far = to_col((0, 1)), to_col((0, 3)), to_col((1, 0))
    up_a = push((0, 0), (0, 3), z_up, 0, HALF)
    down_a = push((0, 0), (0, 1), z_down, HALF, BLOCKS)
    far_a = push((0, 0), (1, 0), x_far, 0, HALF)
    far_b = push((0, 0), (1, 0), x_far, HALF, BLOCKS)
    up_b = push((0, 0), (0, 3), z_up, HALF, BLOCKS)
    down_b = push((0, 0), (0, 1), z_down, 0, HALF)

    def share(rel):
        return remote(block(rel), block(rel, 1), to_col((0, 0), 1))

    shared = {(0, 0): share((0, 0))}

    row_sent = {}
    for i, rel in enumerate(ROW_RELS):
        owner = row_of(rel)
        for k in range(SLOTS):
            tile = send_index[owner, k]
            outgoing[i * SLOTS + k] = own[tile]
        if i:
            there = ROW_RELS.index(back_rel(rel))
            row_sent[back_rel(rel)] = remote(
                outgoing.at[pl.ds(i * SLOTS, SLOTS)],
                arrived.at[pl.ds(there * SLOTS, SLOTS)],
                to_row(rel),
            )

    for b in range(BLOCKS):
        at = pl.ds(b * TILE, TILE)
        back = lax.dot_general(
            weight[...], cotangent[at, :], (((1,), (1,)), ((), ())), preferred_element_type=F32
        )
        pulled[b] = (back * inv_row[b : b + 1, :]).astype(BF16)
        cot_t[:, at] = cotangent[at, :].T

    def mask(hit, live):
        return (hit.astype(jnp.int32) * live).astype(F32)

    def spread_out(marks, lives, store, extra=None):
        def body(b, carry):
            value = mask(marks[0] == b, lives[0]) * prod[0]
            for j in range(1, SLOTS):
                value += mask(marks[j] == b, lives[j]) * prod[j]
            store(b, value)
            return carry

        lax.fori_loop(0, BLOCKS, body, 0)

    def add_to(ref, first=False):
        def store(b, value):
            ref[b] = value if first else ref[b] + value

        return store

    def dense_back(rel, flip):
        base = col_of(rel, flip) * SLOTS
        for j in range(SLOTS):
            prod[j] = jnp.dot(
                pulled[tile_rows[base + j]], tiles[base + j], preferred_element_type=F32
            )
        marks = [tile_cols[base + j] for j in range(SLOTS)]
        lives = [tile_live[base + j] for j in range(SLOTS)]
        return marks, lives

    def place(rel):
        return rel[0] * 4 + rel[1] % 4

    crossed = {}

    def back_cross(rel):
        at = place(rel)

        def store(b, value):
            cross_out[at, b] = value.astype(BF16)

        spread_out(*dense_back(rel, 1), store)
        crossed[rel] = remote(cross_out.at[at], cross_in.at[at], to_col((0, 0), 1))

    def back_own(rel):
        at = place(rel)
        crossed[rel].wait_recv()

        def store(b, value):
            value += cross_in[at, b].astype(F32)
            if rel == (0, 0):
                spread[b] = value
            else:
                sums[at, b] = value.astype(BF16)

        spread_out(*dense_back(rel, 0), store)

    def forward(rel, flip, first=False):
        base = col_of(rel, flip) * SLOTS
        source = block(rel, flip)
        for j in range(SLOTS):
            prod[j] = jnp.dot(
                tiles[base + j], source[tile_cols[base + j]], preferred_element_type=F32
            )
        marks = [tile_rows[base + j] for j in range(SLOTS)]
        lives = [tile_live[base + j] for j in range(SLOTS)]
        spread_out(marks, lives, add_to(gathered, first))

    def remote_forward(i):
        rel = ROW_RELS[i]
        owner = row_of(rel)
        if i:
            row_sent[rel].wait_recv()
        source = arrived if i else outgoing
        for k in range(SLOTS):
            prod[k] = jnp.dot(
                remotes[owner * SLOTS + k], source[i * SLOTS + k], preferred_element_type=F32
            )
        marks = [remote_rows[owner, k] for k in range(SLOTS)]
        lives = [remote_live[owner, k] for k in range(SLOTS)]
        spread_out(marks, lives, add_to(gathered))

    back_sent = {}

    def remote_back(i):
        rel = ROW_RELS[i]
        owner = row_of(rel)
        for k in range(SLOTS):
            value = jnp.dot(
                pulled[remote_rows[owner, k]],
                remotes[owner * SLOTS + k],
                preferred_element_type=F32,
            )
            live = remote_live[owner, k].astype(F32)
            sent_back[i * SLOTS + k] = (value * live).astype(BF16)
        if i:
            there = ROW_RELS.index(back_rel(rel))
            back_sent[back_rel(rel)] = remote(
                sent_back.at[pl.ds(i * SLOTS, SLOTS)],
                returned.at[pl.ds(there * SLOTS, SLOTS)],
                to_row(rel),
            )

    def remote_return(i):
        rel = ROW_RELS[i]
        owner = row_of(rel)
        if i:
            back_sent[rel].wait_recv()
        source = returned if i else sent_back
        for k in range(SLOTS):
            prod[k] = source[i * SLOTS + k].astype(F32)
        marks = [send_index[owner, k] for k in range(SLOTS)]
        spread_out(marks, [jnp.int32(1)] * SLOTS, add_to(spread))

    load_tiles.wait()
    back_cross((1, 2))
    back_cross((1, 1))
    up_a.wait_recv()
    up_c = push((0, 3), (0, 2), z_up, 0, HALF)
    down_a.wait_recv()
    down_c = push((0, 1), (0, 2), z_down, HALF, BLOCKS)
    far_a.wait_recv()
    far_up_a = push((1, 0), (1, 3), z_up, 0, HALF)
    back_cross((1, 3))
    far_b.wait_recv()
    far_down_a = push((1, 0), (1, 1), z_down, HALF, BLOCKS)
    far_up_b = push((1, 0), (1, 3), z_up, HALF, BLOCKS)
    far_down_b = push((1, 0), (1, 1), z_down, 0, HALF)
    shared[1, 0] = share((1, 0))
    up_b.wait_recv()
    shared[0, 3] = share((0, 3))
    down_b.wait_recv()
    shared[0, 1] = share((0, 1))
    load_remotes.wait()
    for i in range(1, len(ROW_RELS)):
        remote_back(i)
    back_cross((1, 0))
    for rel in [(0, 2), (0, 1), (0, 3), (0, 0)]:
        back_cross(rel)
    far_up_a.wait_recv()
    far_up_c = push((1, 3), (1, 2), z_up, 0, HALF)
    far_down_a.wait_recv()
    far_down_c = push((1, 1), (1, 2), z_down, HALF, BLOCKS)
    up_c.wait_recv()
    down_c.wait_recv()
    shared[0, 2] = share((0, 2))
    back_own((1, 2))

    ring = {}

    def ring_start(a):
        ring["up_half", a] = remote(
            sums.at[place((a, 2)), pl.ds(0, HALF)], ring_half.at[a, pl.ds(0, HALF)], z_up
        )
        ring["down_half", a] = remote(
            sums.at[place((a, 2)), pl.ds(HALF, HALF)], ring_half.at[a, pl.ds(HALF, HALF)], z_down
        )

    def ring_early(a):
        ring["up_early", a] = remote(
            sums.at[place((a, 1)), pl.ds(HALF, HALF)], ring_full.at[a, 0, pl.ds(HALF, HALF)], z_up
        )
        ring["down_early", a] = remote(
            sums.at[place((a, 3)), pl.ds(0, HALF)], ring_full.at[a, 1, pl.ds(0, HALF)], z_down
        )

    def ring_late(a):
        for name, rel, lo, side, target in (
            ("up", (a, 1), 0, 0, z_up),
            ("down", (a, 3), HALF, 1, z_down),
        ):
            ring[name + "_half", a].wait_recv()
            at = place(rel)

            def body(b, carry):
                total = sums[at, b].astype(F32) + ring_half[a, b].astype(F32)
                sums[at, b] = total.astype(BF16)
                return carry

            lax.fori_loop(lo, lo + HALF, body, 0)
            ring[name + "_late", a] = remote(
                sums.at[at, pl.ds(lo, HALF)], ring_full.at[a, side, pl.ds(lo, HALF)], target
            )

    ring_start(1)
    back_own((1, 1))
    back_own((1, 3))
    ring_early(1)
    back_own((0, 2))
    ring_start(0)
    back_own((0, 1))
    back_own((0, 3))
    ring_early(0)
    back_own((1, 0))
    back_own((0, 0))

    forward((0, 0), 0, True)
    shared[0, 0].wait_recv()
    forward((0, 0), 1)
    for i in range(len(ROW_RELS)):
        remote_forward(i)
    ring_late(1)
    forward((1, 0), 0)
    forward((0, 1), 0)
    forward((0, 3), 0)
    forward((0, 2), 0)
    for rel in [(1, 0), (0, 1), (0, 3), (0, 2)]:
        shared[rel].wait_recv()
        forward(rel, 1)
    far_up_b.wait_recv()
    shared[1, 3] = share((1, 3))
    far_down_b.wait_recv()
    shared[1, 1] = share((1, 1))
    far_up_c.wait_recv()
    far_down_c.wait_recv()
    shared[1, 2] = share((1, 2))
    ring_late(0)
    for rel in [(1, 3), (1, 1), (1, 2)]:
        forward(rel, 0)
    for rel in [(1, 3), (1, 1), (1, 2)]:
        shared[rel].wait_recv()
        forward(rel, 1)

    total = jnp.zeros((TILE, TILE), F32)
    for b in range(BLOCKS):
        at = pl.ds(b * TILE, TILE)
        hidden = (inv_col[at, :] * gathered[b]).astype(BF16)
        total += jnp.dot(cot_t[:, at], hidden, preferred_element_type=F32)
        out_z[at, :] = jnp.dot(hidden, weight[...], preferred_element_type=F32).astype(BF16)
    wg[...] = total
    half = TILE // 2
    part = half // 8
    mine_half = pl.ds(pl.multiple_of(core * half, half), half)
    other_half = pl.ds(pl.multiple_of((1 - core) * half, half), half)
    halves = remote(wg.at[other_half], wg_core, to_col((0, 0), 1))
    halves.wait_recv()
    wg_part[...] = wg[mine_half, :] + wg_core[...]
    here = x_hi * 4 + z

    def chunk(at):
        return pl.ds(pl.multiple_of(at * part, part), part)

    col_parts = []
    for rel in COL_RELS[1:]:
        there = col_of(rel) // 2
        col_parts.append(remote(wg_part.at[chunk(there)], wg_col.at[here], to_col(rel)))
    wg_col[here] = wg_part[chunk(here), :]

    def pair_send():
        for name in ("up_early", "down_early", "up_late", "down_late"):
            ring[name, 1].wait_recv()
        at = place((1, 0))

        def body(b, carry):
            value = sums[at, b].astype(F32)
            value += ring_full[1, 0, b].astype(F32) + ring_full[1, 1, b].astype(F32)
            pair_out[b] = value.astype(BF16)
            return carry

        lax.fori_loop(0, BLOCKS, body, 0)
        return remote(pair_out, pair_in, x_far)

    for copy in col_parts:
        copy.wait_recv()
    wg_mine[...] = jnp.sum(wg_col[...], axis=0)
    row_parts = []
    for rel in ROW_RELS[1:]:
        row_parts.append(remote(wg_mine, wg_row.at[row], to_row(rel)))
    wg_row[row] = wg_mine[...]
    for i in range(len(ROW_RELS)):
        if i == 0:
            remote_back(0)
        remote_return(i)
    for copy in row_parts:
        copy.wait_recv()
    wg_half[here] = jnp.sum(wg_row[...], axis=0)
    col_full = []
    for rel in COL_RELS[1:]:
        col_full.append(remote(wg_half.at[here], wg_half.at[here], to_col(rel)))
    pair = pair_send()
    for copy in col_full:
        copy.wait_recv()
    full = remote(wg_half, wg_other, to_col((0, 0), 1))
    wg_all[mine_half, :] = wg_half[...].reshape(half, TILE)
    full.wait_recv()
    wg_all[other_half, :] = wg_other[...].reshape(half, TILE)
    grad_w[...] = wg_all[...].T

    for name in ("up_early", "down_early", "up_late", "down_late"):
        ring[name, 0].wait_recv()
    pair.wait_recv()
    for b in range(BLOCKS):
        value = spread[b] + pair_in[b].astype(F32)
        value += ring_full[0, 0, b].astype(F32) + ring_full[0, 1, b].astype(F32)
        value *= inv_row[b : b + 1, :]
        grad_x[pl.ds(b * TILE, TILE), :] = value.T.astype(BF16)
    for copy in copies:
        copy.wait_send()


def on_device(
    features,
    weight,
    cotangent,
    degree,
    tile_vals,
    tile_rows,
    tile_cols,
    tile_live,
    send_index,
    remote_vals,
    remote_rows,
    remote_live,
):
    nodes, width = features.shape
    vmem = pl.BlockSpec(memory_space=pltpu.VMEM)
    smem = pl.BlockSpec(memory_space=pltpu.SMEM)
    hbm = pl.BlockSpec(memory_space=pl.ANY)
    stack = (BLOCKS, TILE, TILE)
    n_copies = 96
    return pl.pallas_call(
        kernel,
        out_shape=(
            jax.ShapeDtypeStruct((nodes, width), BF16),
            jax.ShapeDtypeStruct((nodes, width), BF16),
            jax.ShapeDtypeStruct((TILE, TILE), F32),
        ),
        in_specs=[vmem] * 4 + [smem] * 6 + [hbm] * 2,
        out_specs=(vmem, vmem, vmem),
        scratch_shapes=[
            pltpu.VMEM(tile_vals.shape, BF16),
            pltpu.VMEM(remote_vals.shape, BF16),
            pltpu.VMEM((nodes, TILE), F32),
            pltpu.VMEM(stack, BF16),
            pltpu.VMEM((TILE, nodes), BF16),
            pltpu.VMEM((SLOTS, TILE, TILE), F32),
            pltpu.VMEM(stack, F32),
            pltpu.VMEM(stack, F32),
            pltpu.VMEM((32, TILE, TILE), BF16),
            pltpu.VMEM((32, TILE, TILE), BF16),
            pltpu.VMEM((32, TILE, TILE), BF16),
            pltpu.VMEM((32, TILE, TILE), BF16),
            pltpu.VMEM((8,) + stack, BF16),
            pltpu.VMEM((8,) + stack, BF16),
            pltpu.VMEM((8,) + stack, BF16),
            pltpu.VMEM((2,) + stack, BF16),
            pltpu.VMEM((2, 2) + stack, BF16),
            pltpu.VMEM(stack, BF16),
            pltpu.VMEM(stack, BF16),
            pltpu.VMEM((TILE, TILE), F32),
            pltpu.VMEM((TILE // 2, TILE), F32),
            pltpu.VMEM((TILE // 2, TILE), F32),
            pltpu.VMEM((8, 8, TILE), F32),
            pltpu.VMEM((8, TILE), F32),
            pltpu.VMEM((8, 8, TILE), F32),
            pltpu.VMEM((8, 8, TILE), F32),
            pltpu.VMEM((8, 8, TILE), F32),
            pltpu.VMEM((TILE, TILE), F32),
            pltpu.SemaphoreType.DMA((n_copies,)),
            pltpu.SemaphoreType.DMA((n_copies,)),
            pltpu.SemaphoreType.DMA((2,)),
        ]
        + [pltpu.VMEM(stack, BF16)] * 16,
        compiler_params=pltpu.CompilerParams(
            collective_id=0, has_side_effects=True, vmem_limit_bytes=48 * 2**20
        ),
    )(
        features,
        weight,
        cotangent,
        degree.reshape(BLOCKS, TILE),
        tile_rows,
        tile_cols,
        tile_live,
        send_index,
        remote_rows,
        remote_live,
        tile_vals,
        remote_vals,
    )


def solution(mesh):
    placed = (
        P(("row", "col"), None),
        P(),
        P(("row", "col"), None),
        P(("row", "col")),
        P(("row", "col"), None, None),
        P(("row", "col")),
        P(("row", "col")),
        P(("row", "col")),
        P(("row", "col"), None),
        P(("row", "col"), None, None),
        P(("row", "col"), None),
        P(("row", "col"), None),
    )
    return jax.shard_map(
        on_device,
        mesh=mesh,
        in_specs=placed,
        out_specs=(P(("row", "col"), None), P(("row", "col"), None), P()),
        check_vma=False,
    )
```

```python
import jax
import jax.numpy as jnp
from jax import lax
from jax.experimental import pallas as pl
from jax.experimental.pallas import tpu as pltpu
from jax.sharding import PartitionSpec as P

MESH = pl.DeviceIdType.MESH
BF16 = jnp.bfloat16
F32 = jnp.float32
TILE = 128
BLOCKS = 8
SLOTS = 4
HALF = 4
FIRST = 8
ROW_RELS = [(a, b) for a in range(2) for b in range(4)]
COL_RELS = [(a, b) for a in range(2) for b in range(4)]


def spot():
    row, col = lax.axis_index("row"), lax.axis_index("col")
    return row // 4, row % 4, col // 8, (col // 2) % 4, col % 2


def row_of(rel):
    x_lo, y, _, _, _ = spot()
    return ((x_lo + rel[0]) % 2) * 4 + (y + rel[1]) % 4


def col_of(rel, flip=0):
    _, _, x_hi, z, core = spot()
    return ((x_hi + rel[0]) % 2) * 8 + ((z + rel[1]) % 4) * 2 + (core + flip) % 2


def kernel(
    features_in,
    weight_in,
    cotangent_in,
    degree_in,
    tile_rows_in,
    tile_cols_in,
    tile_live_in,
    send_index_in,
    remote_rows_in,
    remote_live_in,
    tiles_in,
    remotes_in,
    out_z,
    grad_x,
    grad_w,
    features,
    weight,
    cotangent,
    degree,
    tile_rows,
    tile_cols,
    tile_live,
    send_index,
    remote_rows,
    remote_live,
    tiles,
    remotes,
    inv_col,
    pulled,
    cot_t,
    hiddens,
    prod,
    gathered,
    spread,
    outgoing,
    arrived,
    sent_back,
    returned,
    cross_out,
    cross_in,
    sums,
    ring_half,
    ring_full,
    pair_out,
    pair_in,
    wg,
    wg_core,
    wg_part,
    wg_col,
    wg_mine,
    wg_row,
    wg_half,
    wg_other,
    wg_all,
    beside,
    beside_vmem,
    beside_index,
    relayed,
    beside_sum,
    beside_out,
    beside_in,
    turned,
    send_sem,
    recv_sem,
    local_sem,
    *blocks,
):
    row, col = lax.axis_index("row"), lax.axis_index("col")
    _, _, x_hi, z, core = spot()
    copies = []
    arrivals = set()

    def remote(src, dst, target):
        i = len(copies)
        copy = pltpu.make_async_remote_copy(
            src_ref=src,
            dst_ref=dst,
            send_sem=send_sem.at[i],
            recv_sem=recv_sem.at[i],
            device_id=target,
            device_id_type=MESH,
        )
        copies.append(copy)
        copy.start()
        return copy

    def need(*given):
        for copy in given:
            if id(copy) not in arrivals:
                arrivals.add(id(copy))
                copy.wait_recv()

    def to_row(rel):
        return (row_of(rel), col)

    def to_col(rel, flip=0):
        return (row, col_of(rel, flip))

    barrier = pltpu.get_barrier_semaphore()
    peers = [to_col(rel) for rel in COL_RELS[1:]]
    peers += [to_row(rel) for rel in ROW_RELS[1:]]
    peers += [to_col((0, 0), 1)]
    for peer in peers:
        pl.semaphore_signal(barrier, inc=1, device_id=peer, device_id_type=MESH)

    loads = []
    for src, dst in (
        (features_in, features),
        (degree_in, degree),
        (cotangent_in, cotangent),
        (weight_in, weight),
        (send_index_in, send_index),
        (tile_rows_in, tile_rows),
        (tile_cols_in, tile_cols),
        (tile_live_in, tile_live),
        (tiles_in, tiles),
        (remote_rows_in, remote_rows),
        (remote_live_in, remote_live),
        (remotes_in, remotes),
    ):
        load = pltpu.make_async_copy(src, dst, local_sem.at[len(loads)])
        load.start()
        loads.append(load)

    def place(rel):
        return rel[0] * 4 + rel[1] % 4

    def block(rel, flip=0):
        return blocks[place(rel) * 2 + flip]

    own = block((0, 0))
    for load in loads[:2]:
        load.wait()
    inv_row = lax.rsqrt(degree[...].astype(F32))
    for b in range(BLOCKS):
        at = pl.ds(b * TILE, TILE)
        across = jnp.broadcast_to(inv_row[b : b + 1, :], (TILE, TILE)).T
        inv_col[at, :] = across
        own[b] = (features[at, :].astype(F32) * across).astype(BF16)

    def mask(hit, live):
        return (hit.astype(jnp.int32) * live).astype(F32)

    def spread_out(marks, lives, store):
        def body(b):
            value = mask(marks[0] == b, lives[0]) * prod[0]
            for j in range(1, SLOTS):
                value += mask(marks[j] == b, lives[j]) * prod[j]
            store(b, value)

        for b in range(BLOCKS):
            body(b)

    def add_to(ref, first=False):
        def store(b, value):
            ref[b] = value if first else ref[b] + value

        return store

    def dense_back(rel, flip):
        base = col_of(rel, flip) * SLOTS
        for j in range(SLOTS):
            prod[j] = jnp.dot(
                pulled[tile_rows[base + j]], tiles[base + j], preferred_element_type=F32
            )
        marks = [tile_cols[base + j] for j in range(SLOTS)]
        lives = [tile_live[base + j] for j in range(SLOTS)]
        return marks, lives

    crossed = {}

    def cross_make(rel):
        def store(b, value):
            cross_out[place(rel), b] = value.astype(BF16)

        spread_out(*dense_back(rel, 1), store)

    def cross_send(rel):
        at = place(rel)
        crossed[rel] = remote(cross_out.at[at], cross_in.at[at], to_col((0, 0), 1))

    def back_cross(rel):
        cross_make(rel)
        cross_send(rel)

    def back_own(rel):
        at = place(rel)
        need(crossed[rel])

        def store(b, value):
            value += cross_in[at, b].astype(F32)
            if rel == (0, 0):
                spread[b] = value
            else:
                sums[at, b] = value.astype(BF16)

        spread_out(*dense_back(rel, 0), store)

    def forward(rel, flip, first=False):
        base = col_of(rel, flip) * SLOTS
        source = block(rel, flip)
        for j in range(SLOTS):
            prod[j] = jnp.dot(
                tiles[base + j], source[tile_cols[base + j]], preferred_element_type=F32
            )
        marks = [tile_rows[base + j] for j in range(SLOTS)]
        lives = [tile_live[base + j] for j in range(SLOTS)]
        spread_out(marks, lives, add_to(gathered, first))

    def remote_forward(rel):
        i, owner = place(rel), row_of(rel)
        for k in range(SLOTS):
            if rel == (1, 0):
                value = beside[beside_index[k, row]]
            elif rel == (0, 0):
                value = outgoing[k]
            else:
                value = arrived[i * SLOTS + k]
            prod[k] = jnp.dot(remotes[owner * SLOTS + k], value, preferred_element_type=F32)
        marks = [remote_rows[k, owner] for k in range(SLOTS)]
        lives = [remote_live[k, owner] for k in range(SLOTS)]
        spread_out(marks, lives, add_to(gathered))

    def remote_back(rel):
        i, owner = place(rel), row_of(rel)
        for k in range(SLOTS):
            value = jnp.dot(
                pulled[remote_rows[k, owner]],
                remotes[owner * SLOTS + k],
                preferred_element_type=F32,
            )
            live = remote_live[k, owner].astype(F32)
            sent_back[i * SLOTS + k] = (value * live).astype(BF16)

    def returned_sum(side, dy, index, store):
        i = place((side, dy))
        source = returned if dy else sent_back
        for k in range(SLOTS):
            prod[k] = source[i * SLOTS + k].astype(F32)
        marks = [index[k, row_of((0, dy))] for k in range(SLOTS)]
        spread_out(marks, [jnp.int32(1)] * SLOTS, store)

    pl.semaphore_wait(barrier, len(peers))

    z_up, z_down, x_far = to_col((0, 1)), to_col((0, 3)), to_col((1, 0))
    x_near = to_row((1, 0))

    def push(rel_src, rel_dst, target, lo, hi):
        span = pl.ds(lo, hi - lo)
        return remote(block(rel_src).at[span], block(rel_dst).at[span], target)

    shared, mixed, turn, ring, row_sent, back_sent = {}, {}, {}, {}, {}, {}

    def share(rel):
        shared[rel] = remote(block(rel), block(rel, 1), to_col((0, 0), 1))

    def mix(dz):
        if FIRST < BLOCKS:
            mixed[dz] = push((0, dz), (1, dz), x_far, FIRST, BLOCKS)

    def mix_done(dz):
        if FIRST < BLOCKS:
            need(mixed[dz])

    def back_mix(dz):
        if FIRST < BLOCKS:
            turn[dz] = remote(
                sums.at[place((1, dz)), pl.ds(FIRST, BLOCKS - FIRST)],
                turned.at[dz - 1],
                x_far,
            )

    def back_mix_add(dz):
        if FIRST < BLOCKS:
            need(turn[dz])
            at = place((0, dz))
            for b in range(FIRST, BLOCKS):
                total = sums[at, b].astype(F32) + turned[dz - 1, b - FIRST].astype(F32)
                sums[at, b] = total.astype(BF16)

    def row_send(side, dy, source):
        row_sent[side, -dy % 4] = remote(
            source.at[pl.ds(dy * SLOTS, SLOTS)],
            arrived.at[pl.ds(place((side, -dy)) * SLOTS, SLOTS)],
            to_row((0, dy)),
        )

    def back_send(side, dy):
        remote_back((side, dy))
        if dy:
            back_sent[side, -dy % 4] = remote(
                sent_back.at[pl.ds(place((side, dy)) * SLOTS, SLOTS)],
                returned.at[pl.ds(place((side, -dy)) * SLOTS, SLOTS)],
                to_row((0, dy)),
            )

    def send_sums(a, dz, side, lo, hi, target):
        span = pl.ds(lo, hi - lo)
        return remote(sums.at[place((a, dz)), span], ring_full.at[a, side, span], target)

    def ring_start(a, mid, top):
        lower, upper = pl.ds(0, mid), pl.ds(mid, top - mid)
        at = place((a, 2))
        ring["up_half", a] = remote(sums.at[at, lower], ring_half.at[a, lower], z_up)
        ring["down_half", a] = remote(sums.at[at, upper], ring_half.at[a, upper], z_down)
        ring["up_early", a] = send_sums(a, 1, 0, mid, top, z_up)
        ring["down_early", a] = send_sums(a, 3, 1, 0, mid, z_down)

    def ring_late(a, mid, top):
        for name, dz, lo, hi, side, target in (
            ("up", 1, 0, mid, 0, z_up),
            ("down", 3, mid, top, 1, z_down),
        ):
            need(ring[name + "_half", a])
            at = place((a, dz))
            for b in range(lo, hi):
                total = sums[at, b].astype(F32) + ring_half[a, b].astype(F32)
                sums[at, b] = total.astype(BF16)
            ring[name + "_late", a] = send_sums(a, dz, side, lo, hi, target)

    def ring_done(a):
        need(*(ring[name, a] for name in ("up_early", "down_early", "up_late", "down_late")))

    mid = FIRST // 2
    up_a = push((0, 0), (0, 3), z_up, 0, HALF)
    down_a = push((0, 0), (0, 1), z_down, HALF, BLOCKS)
    far_a = push((0, 0), (1, 0), x_far, 0, mid)
    far_b = push((0, 0), (1, 0), x_far, mid, FIRST)
    up_b = push((0, 0), (0, 3), z_up, HALF, BLOCKS)
    down_b = push((0, 0), (0, 1), z_down, 0, HALF)
    near = remote(own, beside, x_near)
    index_near = remote(send_index_in, beside_vmem, x_near)
    far_c = push((0, 0), (1, 0), x_far, FIRST, BLOCKS) if FIRST < BLOCKS else far_b
    loads[4].wait()
    for dy in (1, 3, 2, 0):
        for k in range(SLOTS):
            outgoing[dy * SLOTS + k] = own[send_index[k, row_of((0, dy))]]
        if dy:
            row_send(0, dy, outgoing)
    share((0, 0))

    for load in loads[2:4]:
        load.wait()
    for b in range(BLOCKS):
        at = pl.ds(b * TILE, TILE)
        back = lax.dot_general(
            weight[...], cotangent[at, :], (((1,), (1,)), ((), ())), preferred_element_type=F32
        )
        pulled[b] = (back * inv_row[b : b + 1, :]).astype(BF16)
        cot_t[:, at] = cotangent[at, :].T
    for load in loads[5:]:
        load.wait()

    for rel in [(1, 2), (1, 1), (1, 3)]:
        back_cross(rel)
    need(up_a)
    up_c = push((0, 3), (0, 2), z_up, 0, HALF)
    need(down_a)
    down_c = push((0, 1), (0, 2), z_down, HALF, BLOCKS)
    mix(1)
    for dy in (1, 3):
        back_send(1, dy)
    need(far_a)
    far_up_a = push((1, 0), (1, 3), z_up, 0, mid)
    need(far_b)
    far_down_a = push((1, 0), (1, 1), z_down, mid, FIRST)
    far_up_b = push((1, 0), (1, 3), z_up, mid, FIRST)
    far_down_b = push((1, 0), (1, 1), z_down, 0, mid)
    need(up_b)
    mix(3)
    share((0, 3))
    need(down_b)
    share((0, 1))
    need(far_c)
    share((1, 0))
    for dy in (2, 0):
        back_send(1, dy)
    forward((0, 0), 0, True)
    for rel in [(0, 3), (0, 1), (1, 0)]:
        forward(rel, 0)
    need(down_c)
    mix(2)
    need(up_c)
    share((0, 2))
    for rel in [(0, 2), (0, 1), (0, 3)]:
        back_cross(rel)
    need(shared[0, 0])
    forward((0, 0), 1)
    need(far_up_a)
    far_up_c = push((1, 3), (1, 2), z_up, 0, mid)
    need(far_down_a)
    far_down_c = push((1, 1), (1, 2), z_down, mid, FIRST)

    need(index_near)
    load_index = pltpu.make_async_copy(beside_vmem, beside_index, local_sem.at[len(loads)])
    load_index.start()
    need(near)
    load_index.wait()
    for dy in (1, 3, 2):
        for k in range(SLOTS):
            relayed[dy * SLOTS + k] = beside[beside_index[k, row_of((0, dy))]]
        row_send(1, dy, relayed)
    for rel in [(1, 0), (0, 0)]:
        back_cross(rel)
    for rel in [(1, 2), (1, 1), (1, 3)]:
        back_own(rel)
    ring_start(1, mid, FIRST)
    for dz in (2, 1, 3):
        back_mix(dz)
    need(far_up_b)
    mix_done(3)
    share((1, 3))
    need(far_down_b)
    mix_done(1)
    share((1, 1))
    for rel in [(0, 3), (0, 1), (1, 0)]:
        need(shared[rel])
        forward(rel, 1)
    forward((0, 2), 0)
    need(shared[0, 2])
    forward((0, 2), 1)
    for rel in [(0, 0), (1, 0)]:
        remote_forward(rel)
    for dy in (1, 3, 2):
        need(row_sent[0, dy])
        remote_forward((0, dy))
    for rel in [(1, 3), (1, 1)]:
        forward(rel, 0)
    for rel in [(1, 3), (1, 1)]:
        need(shared[rel])
        forward(rel, 1)
    need(far_up_c, far_down_c)
    mix_done(2)
    share((1, 2))
    forward((1, 2), 0)
    for dy in (1, 3, 2):
        need(row_sent[1, dy])
        remote_forward((1, dy))
    need(shared[1, 2])
    forward((1, 2), 1)

    for b in range(BLOCKS):
        at = pl.ds(b * TILE, TILE)
        hiddens[at, :] = (inv_col[at, :] * gathered[b]).astype(BF16)
    wg[...] = jnp.dot(cot_t[...], hiddens[...], preferred_element_type=F32)
    half = TILE // 2
    part = half // 8
    mine_half = pl.ds(pl.multiple_of(core * half, half), half)
    other_half = pl.ds(pl.multiple_of((1 - core) * half, half), half)
    halves = remote(wg.at[other_half], wg_core, to_col((0, 0), 1))
    here = x_hi * 4 + z

    def chunk(at):
        return pl.ds(pl.multiple_of(at * part, part), part)

    need(halves)
    wg_part[...] = wg[mine_half, :] + wg_core[...]
    col_parts = []
    for rel in COL_RELS[1:]:
        there = col_of(rel) // 2
        col_parts.append(remote(wg_part.at[chunk(there)], wg_col.at[here], to_col(rel)))
    wg_col[here] = wg_part[chunk(here), :]

    ring_late(1, mid, FIRST)
    for rel in [(0, 2), (0, 1), (0, 3)]:
        back_own(rel)
    for dz in (2, 1, 3):
        back_mix_add(dz)
    ring_start(0, HALF, BLOCKS)
    need(*col_parts)
    wg_mine[...] = jnp.sum(wg_col[...], axis=0)
    row_parts = []
    for rel in ROW_RELS[1:]:
        row_parts.append(remote(wg_mine, wg_row.at[row], to_row(rel)))
    wg_row[row] = wg_mine[...]

    for dy in (0, 1, 3, 2):
        if dy:
            need(back_sent[1, dy])
        returned_sum(1, dy, beside_index, add_to(beside_sum, dy == 0))
    for b in range(BLOCKS):
        beside_out[b] = beside_sum[b].astype(BF16)
    beside_sent = remote(beside_out, beside_in, x_near)
    need(*row_parts)
    wg_half[here] = jnp.sum(wg_row[...], axis=0)
    col_full = []
    for rel in COL_RELS[1:]:
        col_full.append(remote(wg_half.at[here], wg_half.at[here], to_col(rel)))

    back_own((1, 0))
    ring_done(1)
    for b in range(BLOCKS):
        value = sums[place((1, 0)), b].astype(F32)
        if b < FIRST:
            value += ring_full[1, 0, b].astype(F32) + ring_full[1, 1, b].astype(F32)
        pair_out[b] = value.astype(BF16)
    pair = remote(pair_out, pair_in, x_far)
    ring_late(0, HALF, BLOCKS)
    for dy in (1, 3, 2, 0):
        back_send(0, dy)
    back_own((0, 0))
    need(*col_full)
    full = remote(wg_half, wg_other, to_col((0, 0), 1))
    wg_all[mine_half, :] = wg_half[...].reshape(half, TILE)
    out_z[...] = jnp.dot(hiddens[...], weight[...], preferred_element_type=F32).astype(BF16)
    need(full)
    wg_all[other_half, :] = wg_other[...].reshape(half, TILE)
    grad_w[...] = wg_all[...].T

    for dy in (0, 1, 3, 2):
        if dy:
            need(back_sent[0, dy])
        returned_sum(0, dy, send_index, add_to(spread))
    need(beside_sent)
    ring_done(0)
    need(pair)
    for b in range(BLOCKS):
        value = spread[b] + pair_in[b].astype(F32) + beside_in[b].astype(F32)
        value += ring_full[0, 0, b].astype(F32) + ring_full[0, 1, b].astype(F32)
        value *= inv_row[b : b + 1, :]
        grad_x[pl.ds(b * TILE, TILE), :] = value.T.astype(BF16)
    for copy in copies:
        copy.wait_send()


def on_device(
    features,
    weight,
    cotangent,
    degree,
    tile_vals,
    tile_rows,
    tile_cols,
    tile_live,
    send_index,
    remote_vals,
    remote_rows,
    remote_live,
):
    nodes, width = features.shape
    vmem = pl.BlockSpec(memory_space=pltpu.VMEM)
    hbm = pl.BlockSpec(memory_space=pl.ANY)
    stack = (BLOCKS, TILE, TILE)
    n_copies = 96
    return pl.pallas_call(
        kernel,
        out_shape=(
            jax.ShapeDtypeStruct((nodes, width), BF16),
            jax.ShapeDtypeStruct((nodes, width), BF16),
            jax.ShapeDtypeStruct((TILE, TILE), F32),
        ),
        in_specs=[hbm] * 12,
        out_specs=(vmem, vmem, vmem),
        scratch_shapes=[
            pltpu.VMEM((nodes, width), BF16),
            pltpu.VMEM(weight.shape, BF16),
            pltpu.VMEM((nodes, width), BF16),
            pltpu.VMEM((BLOCKS, TILE), jnp.int32),
        ]
        + [pltpu.SMEM(tile_rows.shape, jnp.int32)] * 3
        + [pltpu.SMEM(send_index.shape[::-1], jnp.int32)] * 3
        + [
            pltpu.VMEM(tile_vals.shape, BF16),
            pltpu.VMEM(remote_vals.shape, BF16),
            pltpu.VMEM((nodes, TILE), F32),
            pltpu.VMEM(stack, BF16),
            pltpu.VMEM((TILE, nodes), BF16),
            pltpu.VMEM((nodes, TILE), BF16),
            pltpu.VMEM((SLOTS, TILE, TILE), F32),
            pltpu.VMEM(stack, F32),
            pltpu.VMEM(stack, F32),
            pltpu.VMEM((32, TILE, TILE), BF16),
            pltpu.VMEM((32, TILE, TILE), BF16),
            pltpu.VMEM((32, TILE, TILE), BF16),
            pltpu.VMEM((32, TILE, TILE), BF16),
            pltpu.VMEM((8,) + stack, BF16),
            pltpu.VMEM((8,) + stack, BF16),
            pltpu.VMEM((8,) + stack, BF16),
            pltpu.VMEM((2,) + stack, BF16),
            pltpu.VMEM((2, 2) + stack, BF16),
            pltpu.VMEM(stack, BF16),
            pltpu.VMEM(stack, BF16),
            pltpu.VMEM((TILE, TILE), F32),
            pltpu.VMEM((TILE // 2, TILE), F32),
            pltpu.VMEM((TILE // 2, TILE), F32),
            pltpu.VMEM((8, 8, TILE), F32),
            pltpu.VMEM((8, TILE), F32),
            pltpu.VMEM((8, 8, TILE), F32),
            pltpu.VMEM((8, 8, TILE), F32),
            pltpu.VMEM((8, 8, TILE), F32),
            pltpu.VMEM((TILE, TILE), F32),
            pltpu.VMEM(stack, BF16),
            pltpu.VMEM(send_index.shape[::-1], jnp.int32),
            pltpu.SMEM(send_index.shape[::-1], jnp.int32),
            pltpu.VMEM((4 * SLOTS, TILE, TILE), BF16),
            pltpu.VMEM(stack, F32),
            pltpu.VMEM(stack, BF16),
            pltpu.VMEM(stack, BF16),
            pltpu.VMEM((3, max(BLOCKS - FIRST, 1), TILE, TILE), BF16),
            pltpu.SemaphoreType.DMA((n_copies,)),
            pltpu.SemaphoreType.DMA((n_copies,)),
            pltpu.SemaphoreType.DMA((13,)),
        ]
        + [pltpu.VMEM(stack, BF16)] * 16,
        compiler_params=pltpu.CompilerParams(
            collective_id=0, has_side_effects=True, vmem_limit_bytes=63 * 2**20
        ),
    )(
        features,
        weight,
        cotangent,
        degree.reshape(BLOCKS, TILE),
        tile_rows,
        tile_cols,
        tile_live,
        send_index.T,
        remote_rows.T,
        remote_live.T,
        tile_vals,
        remote_vals,
    )


def solution(mesh):
    placed = (
        P(("row", "col"), None),
        P(),
        P(("row", "col"), None),
        P(("row", "col")),
        P(("row", "col"), None, None),
        P(("row", "col")),
        P(("row", "col")),
        P(("row", "col")),
        P(("row", "col"), None),
        P(("row", "col"), None, None),
        P(("row", "col"), None),
        P(("row", "col"), None),
    )
    return jax.shard_map(
        on_device,
        mesh=mesh,
        in_specs=placed,
        out_specs=(P(("row", "col"), None), P(("row", "col"), None), P()),
        check_vma=False,
    )
```

```python
import jax
import jax.numpy as jnp
from jax import lax
from jax.experimental import pallas as pl
from jax.experimental.pallas import tpu as pltpu
from jax.sharding import PartitionSpec as P

MESH = pl.DeviceIdType.MESH
BF16 = jnp.bfloat16
F32 = jnp.float32
TILE = 128
BLOCKS = 8
SLOTS = 4
HALF = 4
FIRST = 8
ROW_RELS = [(a, b) for a in range(2) for b in range(4)]
COL_RELS = [(a, b) for a in range(2) for b in range(4)]


def spot():
    row, col = lax.axis_index("row"), lax.axis_index("col")
    return row // 4, row % 4, col // 8, (col // 2) % 4, col % 2


def row_of(rel):
    x_lo, y, _, _, _ = spot()
    return ((x_lo + rel[0]) % 2) * 4 + (y + rel[1]) % 4


def col_of(rel, flip=0):
    _, _, x_hi, z, core = spot()
    return ((x_hi + rel[0]) % 2) * 8 + ((z + rel[1]) % 4) * 2 + (core + flip) % 2


def kernel(
    features_in,
    weight_in,
    cotangent_in,
    degree_in,
    tile_rows_in,
    tile_cols_in,
    tile_live_in,
    send_index_in,
    remote_rows_in,
    remote_live_in,
    tiles_in,
    remotes_in,
    out_z,
    grad_x,
    grad_w,
    features,
    weight,
    cotangent,
    degree,
    tile_rows,
    tile_cols,
    tile_live,
    send_index,
    remote_rows,
    remote_live,
    tiles,
    remotes,
    inv_col,
    pulled,
    cot_t,
    hiddens,
    prod,
    gathered,
    spread,
    outgoing,
    arrived,
    sent_back,
    returned,
    cross_out,
    cross_in,
    sums,
    ring_half,
    ring_full,
    pair_out,
    pair_in,
    wg,
    wg_core,
    wg_part,
    wg_col,
    wg_mine,
    wg_row,
    wg_half,
    wg_other,
    wg_all,
    beside,
    beside_vmem,
    beside_index,
    relayed,
    beside_sum,
    beside_out,
    beside_in,
    turned,
    send_sem,
    recv_sem,
    local_sem,
    *blocks,
):
    row, col = lax.axis_index("row"), lax.axis_index("col")
    _, _, x_hi, z, core = spot()
    copies = []
    arrivals = set()

    def remote(src, dst, target):
        i = len(copies)
        copy = pltpu.make_async_remote_copy(
            src_ref=src,
            dst_ref=dst,
            send_sem=send_sem.at[i],
            recv_sem=recv_sem.at[i],
            device_id=target,
            device_id_type=MESH,
        )
        copies.append(copy)
        copy.start()
        return copy

    def need(*given):
        for copy in given:
            if id(copy) not in arrivals:
                arrivals.add(id(copy))
                copy.wait_recv()

    def to_row(rel):
        return (row_of(rel), col)

    def to_col(rel, flip=0):
        return (row, col_of(rel, flip))

    barrier = pltpu.get_barrier_semaphore()
    peers = [to_col(rel) for rel in ((0, 1), (0, 3), (1, 0))]
    peers += [to_row(rel) for rel in ((0, 1), (0, 3), (0, 2), (1, 0))]
    peers += [to_col((0, 0), 1)]
    for peer in peers:
        pl.semaphore_signal(barrier, inc=1, device_id=peer, device_id_type=MESH)

    loads = []
    for src, dst in (
        (features_in, features),
        (degree_in, degree),
        (cotangent_in, cotangent),
        (weight_in, weight),
        (send_index_in, send_index),
        (tile_rows_in, tile_rows),
        (tile_cols_in, tile_cols),
        (tile_live_in, tile_live),
        (tiles_in, tiles),
        (remote_rows_in, remote_rows),
        (remote_live_in, remote_live),
        (remotes_in, remotes),
    ):
        load = pltpu.make_async_copy(src, dst, local_sem.at[len(loads)])
        load.start()
        loads.append(load)

    def place(rel):
        return rel[0] * 4 + rel[1] % 4

    def block(rel, flip=0):
        return blocks[place(rel) * 2 + flip]

    own = block((0, 0))
    for load in loads[:2]:
        load.wait()
    inv_row = lax.rsqrt(degree[...].astype(F32))
    for b in range(BLOCKS):
        at = pl.ds(b * TILE, TILE)
        across = jnp.broadcast_to(inv_row[b : b + 1, :], (TILE, TILE)).T
        inv_col[at, :] = across
        own[b] = (features[at, :].astype(F32) * across).astype(BF16)

    def mask(hit, live):
        return (hit.astype(jnp.int32) * live).astype(F32)

    def spread_out(marks, lives, store):
        def body(b):
            value = mask(marks[0] == b, lives[0]) * prod[0]
            for j in range(1, SLOTS):
                value += mask(marks[j] == b, lives[j]) * prod[j]
            store(b, value)

        for b in range(BLOCKS):
            body(b)

    def add_to(ref, first=False):
        def store(b, value):
            ref[b] = value if first else ref[b] + value

        return store

    def dense_back(rel, flip):
        base = col_of(rel, flip) * SLOTS
        for j in range(SLOTS):
            prod[j] = jnp.dot(
                pulled[tile_rows[base + j]], tiles[base + j], preferred_element_type=F32
            )
        marks = [tile_cols[base + j] for j in range(SLOTS)]
        lives = [tile_live[base + j] for j in range(SLOTS)]
        return marks, lives

    crossed = {}

    def cross_make(rel):
        def store(b, value):
            cross_out[place(rel), b] = value.astype(BF16)

        spread_out(*dense_back(rel, 1), store)

    def cross_send(rel):
        at = place(rel)
        crossed[rel] = remote(cross_out.at[at], cross_in.at[at], to_col((0, 0), 1))

    def back_cross(rel):
        cross_make(rel)
        cross_send(rel)

    def back_own(rel):
        at = place(rel)
        need(crossed[rel])

        def store(b, value):
            value += cross_in[at, b].astype(F32)
            if rel == (0, 0):
                spread[b] = value
            else:
                sums[at, b] = value.astype(BF16)

        spread_out(*dense_back(rel, 0), store)

    def forward(rel, flip, first=False):
        base = col_of(rel, flip) * SLOTS
        source = block(rel, flip)
        for j in range(SLOTS):
            prod[j] = jnp.dot(
                tiles[base + j], source[tile_cols[base + j]], preferred_element_type=F32
            )
        marks = [tile_rows[base + j] for j in range(SLOTS)]
        lives = [tile_live[base + j] for j in range(SLOTS)]
        spread_out(marks, lives, add_to(gathered, first))

    def remote_forward(rel):
        i, owner = place(rel), row_of(rel)
        for k in range(SLOTS):
            if rel == (1, 0):
                value = beside[beside_index[k, row]]
            elif rel == (0, 0):
                value = outgoing[k]
            else:
                value = arrived[i * SLOTS + k]
            prod[k] = jnp.dot(remotes[owner * SLOTS + k], value, preferred_element_type=F32)
        marks = [remote_rows[k, owner] for k in range(SLOTS)]
        lives = [remote_live[k, owner] for k in range(SLOTS)]
        spread_out(marks, lives, add_to(gathered))

    def remote_back(rel):
        i, owner = place(rel), row_of(rel)
        for k in range(SLOTS):
            value = jnp.dot(
                pulled[remote_rows[k, owner]],
                remotes[owner * SLOTS + k],
                preferred_element_type=F32,
            )
            live = remote_live[k, owner].astype(F32)
            sent_back[i * SLOTS + k] = (value * live).astype(BF16)

    def returned_sum(side, dy, index, store):
        i = place((side, dy))
        source = returned if dy else sent_back
        for k in range(SLOTS):
            prod[k] = source[i * SLOTS + k].astype(F32)
        marks = [index[k, row_of((0, dy))] for k in range(SLOTS)]
        spread_out(marks, [jnp.int32(1)] * SLOTS, store)

    pl.semaphore_wait(barrier, len(peers))

    z_up, z_down, x_far = to_col((0, 1)), to_col((0, 3)), to_col((1, 0))
    x_near = to_row((1, 0))

    def push(rel_src, rel_dst, target, lo, hi):
        span = pl.ds(lo, hi - lo)
        return remote(block(rel_src).at[span], block(rel_dst).at[span], target)

    shared, mixed, turn, ring, row_sent, back_sent = {}, {}, {}, {}, {}, {}

    def share(rel):
        shared[rel] = remote(block(rel), block(rel, 1), to_col((0, 0), 1))

    def mix(dz):
        if FIRST < BLOCKS:
            mixed[dz] = push((0, dz), (1, dz), x_far, FIRST, BLOCKS)

    def mix_done(dz):
        if FIRST < BLOCKS:
            need(mixed[dz])

    def back_mix(dz):
        if FIRST < BLOCKS:
            turn[dz] = remote(
                sums.at[place((1, dz)), pl.ds(FIRST, BLOCKS - FIRST)],
                turned.at[dz - 1],
                x_far,
            )

    def back_mix_add(dz):
        if FIRST < BLOCKS:
            need(turn[dz])
            at = place((0, dz))
            for b in range(FIRST, BLOCKS):
                total = sums[at, b].astype(F32) + turned[dz - 1, b - FIRST].astype(F32)
                sums[at, b] = total.astype(BF16)

    def row_send(side, dy, source):
        row_sent[side, -dy % 4] = remote(
            source.at[pl.ds(dy * SLOTS, SLOTS)],
            arrived.at[pl.ds(place((side, -dy)) * SLOTS, SLOTS)],
            to_row((0, dy)),
        )

    def back_send(side, dy):
        remote_back((side, dy))
        if dy:
            back_sent[side, -dy % 4] = remote(
                sent_back.at[pl.ds(place((side, dy)) * SLOTS, SLOTS)],
                returned.at[pl.ds(place((side, -dy)) * SLOTS, SLOTS)],
                to_row((0, dy)),
            )

    def send_sums(a, dz, side, lo, hi, target):
        span = pl.ds(lo, hi - lo)
        return remote(sums.at[place((a, dz)), span], ring_full.at[a, side, span], target)

    def ring_start(a, mid, top):
        lower, upper = pl.ds(0, mid), pl.ds(mid, top - mid)
        at = place((a, 2))
        ring["up_half", a] = remote(sums.at[at, lower], ring_half.at[a, lower], z_up)
        ring["down_half", a] = remote(sums.at[at, upper], ring_half.at[a, upper], z_down)
        ring["up_early", a] = send_sums(a, 1, 0, mid, top, z_up)
        ring["down_early", a] = send_sums(a, 3, 1, 0, mid, z_down)

    def ring_late(a, mid, top):
        for name, dz, lo, hi, side, target in (
            ("up", 1, 0, mid, 0, z_up),
            ("down", 3, mid, top, 1, z_down),
        ):
            need(ring[name + "_half", a])
            at = place((a, dz))
            for b in range(lo, hi):
                total = sums[at, b].astype(F32) + ring_half[a, b].astype(F32)
                sums[at, b] = total.astype(BF16)
            ring[name + "_late", a] = send_sums(a, dz, side, lo, hi, target)

    def ring_done(a):
        need(*(ring[name, a] for name in ("up_early", "down_early", "up_late", "down_late")))

    mid = FIRST // 2
    up_a = push((0, 0), (0, 3), z_up, 0, HALF)
    down_a = push((0, 0), (0, 1), z_down, HALF, BLOCKS)
    far_a = push((0, 0), (1, 0), x_far, 0, mid)
    far_b = push((0, 0), (1, 0), x_far, mid, FIRST)
    up_b = push((0, 0), (0, 3), z_up, HALF, BLOCKS)
    down_b = push((0, 0), (0, 1), z_down, 0, HALF)
    near = remote(own, beside, x_near)
    index_near = remote(send_index_in, beside_vmem, x_near)
    far_c = push((0, 0), (1, 0), x_far, FIRST, BLOCKS) if FIRST < BLOCKS else far_b
    loads[4].wait()
    for dy in (1, 3, 2, 0):
        for k in range(SLOTS):
            outgoing[dy * SLOTS + k] = own[send_index[k, row_of((0, dy))]]
        if dy:
            row_send(0, dy, outgoing)
    share((0, 0))

    for load in loads[2:4]:
        load.wait()
    for b in range(BLOCKS):
        at = pl.ds(b * TILE, TILE)
        back = lax.dot_general(
            weight[...], cotangent[at, :], (((1,), (1,)), ((), ())), preferred_element_type=F32
        )
        pulled[b] = (back * inv_row[b : b + 1, :]).astype(BF16)
        cot_t[:, at] = cotangent[at, :].T
    for load in loads[5:]:
        load.wait()

    for rel in [(1, 2), (1, 1), (1, 3)]:
        back_cross(rel)
    need(up_a)
    up_c = push((0, 3), (0, 2), z_up, 0, HALF)
    need(down_a)
    down_c = push((0, 1), (0, 2), z_down, HALF, BLOCKS)
    mix(1)
    for dy in (1, 3):
        back_send(1, dy)
    need(far_a)
    far_up_a = push((1, 0), (1, 3), z_up, 0, mid)
    need(far_b)
    far_down_a = push((1, 0), (1, 1), z_down, mid, FIRST)
    far_up_b = push((1, 0), (1, 3), z_up, mid, FIRST)
    far_down_b = push((1, 0), (1, 1), z_down, 0, mid)
    need(up_b)
    mix(3)
    share((0, 3))
    need(down_b)
    share((0, 1))
    need(far_c)
    share((1, 0))
    for dy in (2, 0):
        back_send(1, dy)
    forward((0, 0), 0, True)
    for rel in [(0, 3), (0, 1), (1, 0)]:
        forward(rel, 0)
    need(down_c)
    mix(2)
    need(up_c)
    share((0, 2))
    for rel in [(0, 2), (0, 1), (0, 3)]:
        back_cross(rel)
    need(shared[0, 0])
    forward((0, 0), 1)
    need(far_up_a)
    far_up_c = push((1, 3), (1, 2), z_up, 0, mid)
    need(far_down_a)
    far_down_c = push((1, 1), (1, 2), z_down, mid, FIRST)

    need(index_near)
    load_index = pltpu.make_async_copy(beside_vmem, beside_index, local_sem.at[len(loads)])
    load_index.start()
    need(near)
    load_index.wait()
    for dy in (1, 3, 2):
        for k in range(SLOTS):
            relayed[dy * SLOTS + k] = beside[beside_index[k, row_of((0, dy))]]
        row_send(1, dy, relayed)
    for rel in [(1, 0), (0, 0)]:
        back_cross(rel)
    for rel in [(1, 2), (1, 1), (1, 3)]:
        back_own(rel)
    ring_start(1, mid, FIRST)
    for dz in (2, 1, 3):
        back_mix(dz)
    need(far_up_b)
    mix_done(3)
    share((1, 3))
    need(far_down_b)
    mix_done(1)
    share((1, 1))
    for rel in [(0, 3), (0, 1), (1, 0)]:
        need(shared[rel])
        forward(rel, 1)
    forward((0, 2), 0)
    need(shared[0, 2])
    forward((0, 2), 1)
    for rel in [(0, 0), (1, 0)]:
        remote_forward(rel)
    for dy in (1, 3, 2):
        need(row_sent[0, dy])
        remote_forward((0, dy))
    for rel in [(1, 3), (1, 1)]:
        forward(rel, 0)
    for rel in [(1, 3), (1, 1)]:
        need(shared[rel])
        forward(rel, 1)
    for dy in (0, 1, 3, 2):
        if dy:
            need(back_sent[1, dy])
        returned_sum(1, dy, beside_index, add_to(beside_sum, dy == 0))
    for b in range(BLOCKS):
        beside_out[b] = beside_sum[b].astype(BF16)
    beside_sent = remote(beside_out, beside_in, x_near)
    need(far_up_c, far_down_c)
    mix_done(2)
    share((1, 2))
    forward((1, 2), 0)
    for dy in (1, 3, 2):
        need(row_sent[1, dy])
        remote_forward((1, dy))
    need(shared[1, 2])
    forward((1, 2), 1)

    for b in range(BLOCKS):
        at = pl.ds(b * TILE, TILE)
        hiddens[at, :] = (inv_col[at, :] * gathered[b]).astype(BF16)
    wg[...] = jnp.dot(cot_t[...], hiddens[...], preferred_element_type=F32)
    half = TILE // 2
    part = half // 8
    mine_half = pl.ds(pl.multiple_of(core * half, half), half)
    other_half = pl.ds(pl.multiple_of((1 - core) * half, half), half)
    halves = remote(wg.at[other_half], wg_core, to_col((0, 0), 1))
    here = x_hi * 4 + z

    def chunk(at):
        return pl.ds(pl.multiple_of(at * part, part), part)

    need(halves)
    wg_part[...] = wg[mine_half, :] + wg_core[...]
    col_parts = []
    for rel in COL_RELS[1:]:
        there = col_of(rel) // 2
        col_parts.append(remote(wg_part.at[chunk(there)], wg_col.at[here], to_col(rel)))
    wg_col[here] = wg_part[chunk(here), :]

    ring_late(1, mid, FIRST)
    for rel in [(0, 2), (0, 1), (0, 3)]:
        back_own(rel)
    for dz in (2, 1, 3):
        back_mix_add(dz)
    ring_start(0, HALF, BLOCKS)
    for dy in (1, 3, 2, 0):
        back_send(0, dy)
    need(*col_parts)
    wg_mine[...] = jnp.sum(wg_col[...], axis=0)
    row_parts = []
    for rel in ROW_RELS[1:]:
        row_parts.append(remote(wg_mine, wg_row.at[row], to_row(rel)))
    wg_row[row] = wg_mine[...]

    need(*row_parts)
    wg_half[here] = jnp.sum(wg_row[...], axis=0)
    col_full = []
    for rel in COL_RELS[1:]:
        col_full.append(remote(wg_half.at[here], wg_half.at[here], to_col(rel)))

    back_own((1, 0))
    ring_done(1)
    for b in range(BLOCKS):
        value = sums[place((1, 0)), b].astype(F32)
        if b < FIRST:
            value += ring_full[1, 0, b].astype(F32) + ring_full[1, 1, b].astype(F32)
        pair_out[b] = value.astype(BF16)
    pair = remote(pair_out, pair_in, x_far)
    ring_late(0, HALF, BLOCKS)
    back_own((0, 0))
    need(*col_full)
    full = remote(wg_half, wg_other, to_col((0, 0), 1))
    wg_all[mine_half, :] = wg_half[...].reshape(half, TILE)
    out_z[...] = jnp.dot(hiddens[...], weight[...], preferred_element_type=F32).astype(BF16)
    need(full)
    wg_all[other_half, :] = wg_other[...].reshape(half, TILE)
    grad_w[...] = wg_all[...].T

    for dy in (0, 1, 3, 2):
        if dy:
            need(back_sent[0, dy])
        returned_sum(0, dy, send_index, add_to(spread))
    need(beside_sent)
    ring_done(0)
    need(pair)
    for b in range(BLOCKS):
        value = spread[b] + pair_in[b].astype(F32) + beside_in[b].astype(F32)
        value += ring_full[0, 0, b].astype(F32) + ring_full[0, 1, b].astype(F32)
        value *= inv_row[b : b + 1, :]
        grad_x[pl.ds(b * TILE, TILE), :] = value.T.astype(BF16)
    for copy in copies:
        copy.wait_send()


def on_device(
    features,
    weight,
    cotangent,
    degree,
    tile_vals,
    tile_rows,
    tile_cols,
    tile_live,
    send_index,
    remote_vals,
    remote_rows,
    remote_live,
):
    nodes, width = features.shape
    vmem = pl.BlockSpec(memory_space=pltpu.VMEM)
    hbm = pl.BlockSpec(memory_space=pl.ANY)
    stack = (BLOCKS, TILE, TILE)
    n_copies = 96
    return pl.pallas_call(
        kernel,
        out_shape=(
            jax.ShapeDtypeStruct((nodes, width), BF16),
            jax.ShapeDtypeStruct((nodes, width), BF16),
            jax.ShapeDtypeStruct((TILE, TILE), F32),
        ),
        in_specs=[hbm] * 12,
        out_specs=(vmem, vmem, vmem),
        scratch_shapes=[
            pltpu.VMEM((nodes, width), BF16),
            pltpu.VMEM(weight.shape, BF16),
            pltpu.VMEM((nodes, width), BF16),
            pltpu.VMEM((BLOCKS, TILE), jnp.int32),
        ]
        + [pltpu.SMEM(tile_rows.shape, jnp.int32)] * 3
        + [pltpu.SMEM(send_index.shape[::-1], jnp.int32)] * 3
        + [
            pltpu.VMEM(tile_vals.shape, BF16),
            pltpu.VMEM(remote_vals.shape, BF16),
            pltpu.VMEM((nodes, TILE), F32),
            pltpu.VMEM(stack, BF16),
            pltpu.VMEM((TILE, nodes), BF16),
            pltpu.VMEM((nodes, TILE), BF16),
            pltpu.VMEM((SLOTS, TILE, TILE), F32),
            pltpu.VMEM(stack, F32),
            pltpu.VMEM(stack, F32),
            pltpu.VMEM((32, TILE, TILE), BF16),
            pltpu.VMEM((32, TILE, TILE), BF16),
            pltpu.VMEM((32, TILE, TILE), BF16),
            pltpu.VMEM((32, TILE, TILE), BF16),
            pltpu.VMEM((8,) + stack, BF16),
            pltpu.VMEM((8,) + stack, BF16),
            pltpu.VMEM((8,) + stack, BF16),
            pltpu.VMEM((2,) + stack, BF16),
            pltpu.VMEM((2, 2) + stack, BF16),
            pltpu.VMEM(stack, BF16),
            pltpu.VMEM(stack, BF16),
            pltpu.VMEM((TILE, TILE), F32),
            pltpu.VMEM((TILE // 2, TILE), F32),
            pltpu.VMEM((TILE // 2, TILE), F32),
            pltpu.VMEM((8, 8, TILE), F32),
            pltpu.VMEM((8, TILE), F32),
            pltpu.VMEM((8, 8, TILE), F32),
            pltpu.VMEM((8, 8, TILE), F32),
            pltpu.VMEM((8, 8, TILE), F32),
            pltpu.VMEM((TILE, TILE), F32),
            pltpu.VMEM(stack, BF16),
            pltpu.VMEM(send_index.shape[::-1], jnp.int32),
            pltpu.SMEM(send_index.shape[::-1], jnp.int32),
            pltpu.VMEM((4 * SLOTS, TILE, TILE), BF16),
            pltpu.VMEM(stack, F32),
            pltpu.VMEM(stack, BF16),
            pltpu.VMEM(stack, BF16),
            pltpu.VMEM((3, max(BLOCKS - FIRST, 1), TILE, TILE), BF16),
            pltpu.SemaphoreType.DMA((n_copies,)),
            pltpu.SemaphoreType.DMA((n_copies,)),
            pltpu.SemaphoreType.DMA((13,)),
        ]
        + [pltpu.VMEM(stack, BF16)] * 16,
        compiler_params=pltpu.CompilerParams(
            collective_id=0, has_side_effects=True, vmem_limit_bytes=63 * 2**20
        ),
    )(
        features,
        weight,
        cotangent,
        degree.reshape(BLOCKS, TILE),
        tile_rows,
        tile_cols,
        tile_live,
        send_index.T,
        remote_rows.T,
        remote_live.T,
        tile_vals,
        remote_vals,
    )


def solution(mesh):
    placed = (
        P(("row", "col"), None),
        P(),
        P(("row", "col"), None),
        P(("row", "col")),
        P(("row", "col"), None, None),
        P(("row", "col")),
        P(("row", "col")),
        P(("row", "col")),
        P(("row", "col"), None),
        P(("row", "col"), None, None),
        P(("row", "col"), None),
        P(("row", "col"), None),
    )
    return jax.shard_map(
        on_device,
        mesh=mesh,
        in_specs=placed,
        out_specs=(P(("row", "col"), None), P(("row", "col"), None), P()),
        check_vma=False,
    )
```

```python
import jax
import jax.numpy as jnp
from jax import lax
from jax.experimental import pallas as pl
from jax.experimental.pallas import tpu as pltpu
from jax.sharding import PartitionSpec as P

MESH = pl.DeviceIdType.MESH
BF16 = jnp.bfloat16
F32 = jnp.float32
TILE = 128
BLOCKS = 8
SLOTS = 4
HALF = 4
FIRST = 8
ROW_RELS = [(a, b) for a in range(2) for b in range(4)]
COL_RELS = [(a, b) for a in range(2) for b in range(4)]


def spot():
    row, col = lax.axis_index("row"), lax.axis_index("col")
    return row // 4, row % 4, col // 8, (col // 2) % 4, col % 2


def row_of(rel):
    x_lo, y, _, _, _ = spot()
    return ((x_lo + rel[0]) % 2) * 4 + (y + rel[1]) % 4


def col_of(rel, flip=0):
    _, _, x_hi, z, core = spot()
    return ((x_hi + rel[0]) % 2) * 8 + ((z + rel[1]) % 4) * 2 + (core + flip) % 2


def kernel(
    features_in,
    weight_in,
    cotangent_in,
    degree_in,
    tile_rows_in,
    tile_cols_in,
    tile_live_in,
    send_index_in,
    remote_rows_in,
    remote_live_in,
    tiles_in,
    remotes_in,
    out_z_out,
    grad_x_out,
    grad_w_out,
    out_z,
    grad_x,
    grad_w,
    features,
    weight,
    cotangent,
    degree,
    tile_rows,
    tile_cols,
    tile_live,
    send_index,
    remote_rows,
    remote_live,
    tiles,
    remotes,
    inv_col,
    pulled,
    cot_t,
    hiddens,
    prod,
    gathered,
    spread,
    outgoing,
    arrived,
    sent_back,
    returned,
    cross_out,
    cross_in,
    sums,
    ring_half,
    ring_full,
    pair_out,
    pair_in,
    wg,
    wg_core,
    wg_part,
    wg_col,
    wg_mine,
    wg_row,
    wg_half,
    wg_other,
    wg_all,
    beside,
    beside_vmem,
    beside_index,
    relayed,
    beside_sum,
    beside_out,
    beside_in,
    turned,
    send_sem,
    recv_sem,
    local_sem,
    *blocks,
):
    row, col = lax.axis_index("row"), lax.axis_index("col")
    _, _, x_hi, z, core = spot()
    copies = []
    arrivals = set()

    def remote(src, dst, target):
        i = len(copies)
        copy = pltpu.make_async_remote_copy(
            src_ref=src,
            dst_ref=dst,
            send_sem=send_sem.at[i],
            recv_sem=recv_sem.at[i],
            device_id=target,
            device_id_type=MESH,
        )
        copies.append(copy)
        copy.start()
        return copy

    def need(*given):
        for copy in given:
            if id(copy) not in arrivals:
                arrivals.add(id(copy))
                copy.wait_recv()

    def to_row(rel):
        return (row_of(rel), col)

    def to_col(rel, flip=0):
        return (row, col_of(rel, flip))

    barrier = pltpu.get_barrier_semaphore()
    peers = [to_col(rel) for rel in ((0, 1), (0, 3), (1, 0))]
    peers += [to_row(rel) for rel in ((0, 1), (0, 3), (0, 2), (1, 0))]
    peers += [to_col((0, 0), 1)]
    for peer in peers:
        pl.semaphore_signal(barrier, inc=1, device_id=peer, device_id_type=MESH)

    loads = []
    for src, dst in (
        (features_in, features),
        (degree_in, degree),
        (cotangent_in, cotangent),
        (weight_in, weight),
        (send_index_in, send_index),
        (tile_rows_in, tile_rows),
        (tile_cols_in, tile_cols),
        (tile_live_in, tile_live),
        (tiles_in, tiles),
        (remote_rows_in, remote_rows),
        (remote_live_in, remote_live),
        (remotes_in, remotes),
    ):
        load = pltpu.make_async_copy(src, dst, local_sem.at[len(loads)])
        load.start()
        loads.append(load)

    def place(rel):
        return rel[0] * 4 + rel[1] % 4

    def block(rel, flip=0):
        return blocks[place(rel) * 2 + flip]

    own = block((0, 0))
    for load in loads[:2]:
        load.wait()
    inv_row = lax.rsqrt(degree[...].astype(F32))
    for b in range(BLOCKS):
        at = pl.ds(b * TILE, TILE)
        across = jnp.broadcast_to(inv_row[b : b + 1, :], (TILE, TILE)).T
        inv_col[at, :] = across
        own[b] = (features[at, :].astype(F32) * across).astype(BF16)

    def mask(hit, live):
        return (hit.astype(jnp.int32) * live).astype(F32)

    def spread_out(marks, lives, store):
        def body(b):
            value = mask(marks[0] == b, lives[0]) * prod[0]
            for j in range(1, SLOTS):
                value += mask(marks[j] == b, lives[j]) * prod[j]
            store(b, value)

        for b in range(BLOCKS):
            body(b)

    def add_to(ref, first=False):
        def store(b, value):
            ref[b] = value if first else ref[b] + value

        return store

    def dense_back(rel, flip):
        base = col_of(rel, flip) * SLOTS
        for j in range(SLOTS):
            prod[j] = jnp.dot(
                pulled[tile_rows[base + j]], tiles[base + j], preferred_element_type=F32
            )
        marks = [tile_cols[base + j] for j in range(SLOTS)]
        lives = [tile_live[base + j] for j in range(SLOTS)]
        return marks, lives

    crossed = {}

    def cross_make(rel):
        def store(b, value):
            cross_out[place(rel), b] = value.astype(BF16)

        spread_out(*dense_back(rel, 1), store)

    def cross_send(rel):
        at = place(rel)
        crossed[rel] = remote(cross_out.at[at], cross_in.at[at], to_col((0, 0), 1))

    def back_cross(rel):
        cross_make(rel)
        cross_send(rel)

    def back_own(rel):
        at = place(rel)
        need(crossed[rel])

        def store(b, value):
            value += cross_in[at, b].astype(F32)
            if rel == (0, 0):
                spread[b] = value
            else:
                sums[at, b] = value.astype(BF16)

        spread_out(*dense_back(rel, 0), store)

    def forward(rel, flip, first=False):
        base = col_of(rel, flip) * SLOTS
        source = block(rel, flip)
        for j in range(SLOTS):
            prod[j] = jnp.dot(
                tiles[base + j], source[tile_cols[base + j]], preferred_element_type=F32
            )
        marks = [tile_rows[base + j] for j in range(SLOTS)]
        lives = [tile_live[base + j] for j in range(SLOTS)]
        spread_out(marks, lives, add_to(gathered, first))

    def remote_forward(rel):
        i, owner = place(rel), row_of(rel)
        for k in range(SLOTS):
            if rel == (1, 0):
                value = beside[beside_index[k, row]]
            elif rel == (0, 0):
                value = outgoing[k]
            else:
                value = arrived[i * SLOTS + k]
            prod[k] = jnp.dot(remotes[owner * SLOTS + k], value, preferred_element_type=F32)
        marks = [remote_rows[k, owner] for k in range(SLOTS)]
        lives = [remote_live[k, owner] for k in range(SLOTS)]
        spread_out(marks, lives, add_to(gathered))

    def remote_back(rel):
        i, owner = place(rel), row_of(rel)
        for k in range(SLOTS):
            value = jnp.dot(
                pulled[remote_rows[k, owner]],
                remotes[owner * SLOTS + k],
                preferred_element_type=F32,
            )
            live = remote_live[k, owner].astype(F32)
            sent_back[i * SLOTS + k] = (value * live).astype(BF16)

    def returned_sum(side, dy, index, store):
        i = place((side, dy))
        source = returned if dy else sent_back
        for k in range(SLOTS):
            prod[k] = source[i * SLOTS + k].astype(F32)
        marks = [index[k, row_of((0, dy))] for k in range(SLOTS)]
        spread_out(marks, [jnp.int32(1)] * SLOTS, store)

    pl.semaphore_wait(barrier, len(peers))

    z_up, z_down, x_far = to_col((0, 1)), to_col((0, 3)), to_col((1, 0))
    x_near = to_row((1, 0))

    def push(rel_src, rel_dst, target, lo, hi):
        span = pl.ds(lo, hi - lo)
        return remote(block(rel_src).at[span], block(rel_dst).at[span], target)

    shared, mixed, turn, ring, row_sent, back_sent = {}, {}, {}, {}, {}, {}

    def share(rel):
        shared[rel] = remote(block(rel), block(rel, 1), to_col((0, 0), 1))

    def mix(dz):
        if FIRST < BLOCKS:
            mixed[dz] = push((0, dz), (1, dz), x_far, FIRST, BLOCKS)

    def mix_done(dz):
        if FIRST < BLOCKS:
            need(mixed[dz])

    def back_mix(dz):
        if FIRST < BLOCKS:
            turn[dz] = remote(
                sums.at[place((1, dz)), pl.ds(FIRST, BLOCKS - FIRST)],
                turned.at[dz - 1],
                x_far,
            )

    def back_mix_add(dz):
        if FIRST < BLOCKS:
            need(turn[dz])
            at = place((0, dz))
            for b in range(FIRST, BLOCKS):
                total = sums[at, b].astype(F32) + turned[dz - 1, b - FIRST].astype(F32)
                sums[at, b] = total.astype(BF16)

    def row_send(side, dy, source):
        row_sent[side, -dy % 4] = remote(
            source.at[pl.ds(dy * SLOTS, SLOTS)],
            arrived.at[pl.ds(place((side, -dy)) * SLOTS, SLOTS)],
            to_row((0, dy)),
        )

    def back_send(side, dy):
        remote_back((side, dy))
        if dy:
            back_sent[side, -dy % 4] = remote(
                sent_back.at[pl.ds(place((side, dy)) * SLOTS, SLOTS)],
                returned.at[pl.ds(place((side, -dy)) * SLOTS, SLOTS)],
                to_row((0, dy)),
            )

    def send_sums(a, dz, side, lo, hi, target):
        span = pl.ds(lo, hi - lo)
        return remote(sums.at[place((a, dz)), span], ring_full.at[a, side, span], target)

    def ring_start(a, mid, top):
        lower, upper = pl.ds(0, mid), pl.ds(mid, top - mid)
        at = place((a, 2))
        ring["up_half", a] = remote(sums.at[at, lower], ring_half.at[a, lower], z_up)
        ring["down_half", a] = remote(sums.at[at, upper], ring_half.at[a, upper], z_down)
        ring["up_early", a] = send_sums(a, 1, 0, mid, top, z_up)
        ring["down_early", a] = send_sums(a, 3, 1, 0, mid, z_down)

    def ring_late(a, mid, top):
        for name, dz, lo, hi, side, target in (
            ("up", 1, 0, mid, 0, z_up),
            ("down", 3, mid, top, 1, z_down),
        ):
            need(ring[name + "_half", a])
            at = place((a, dz))
            for b in range(lo, hi):
                total = sums[at, b].astype(F32) + ring_half[a, b].astype(F32)
                sums[at, b] = total.astype(BF16)
            ring[name + "_late", a] = send_sums(a, dz, side, lo, hi, target)

    def ring_done(a):
        need(*(ring[name, a] for name in ("up_early", "down_early", "up_late", "down_late")))

    mid = FIRST // 2
    up_a = push((0, 0), (0, 3), z_up, 0, HALF)
    down_a = push((0, 0), (0, 1), z_down, HALF, BLOCKS)
    far_a = push((0, 0), (1, 0), x_far, 0, mid)
    far_b = push((0, 0), (1, 0), x_far, mid, FIRST)
    up_b = push((0, 0), (0, 3), z_up, HALF, BLOCKS)
    down_b = push((0, 0), (0, 1), z_down, 0, HALF)
    near = remote(own, beside, x_near)
    index_near = remote(send_index_in, beside_vmem, x_near)
    far_c = push((0, 0), (1, 0), x_far, FIRST, BLOCKS) if FIRST < BLOCKS else far_b
    loads[4].wait()
    for dy in (1, 3, 2, 0):
        for k in range(SLOTS):
            outgoing[dy * SLOTS + k] = own[send_index[k, row_of((0, dy))]]
        if dy:
            row_send(0, dy, outgoing)
    share((0, 0))

    for load in loads[2:4]:
        load.wait()
    for b in range(BLOCKS):
        at = pl.ds(b * TILE, TILE)
        back = lax.dot_general(
            weight[...], cotangent[at, :], (((1,), (1,)), ((), ())), preferred_element_type=F32
        )
        pulled[b] = (back * inv_row[b : b + 1, :]).astype(BF16)
        cot_t[:, at] = cotangent[at, :].T
    for load in loads[5:]:
        load.wait()

    for rel in [(1, 2), (1, 1), (1, 3)]:
        back_cross(rel)
    need(up_a)
    up_c = push((0, 3), (0, 2), z_up, 0, HALF)
    need(down_a)
    down_c = push((0, 1), (0, 2), z_down, HALF, BLOCKS)
    mix(1)
    for dy in (1, 3):
        back_send(1, dy)
    need(far_a)
    far_up_a = push((1, 0), (1, 3), z_up, 0, mid)
    need(far_b)
    far_down_a = push((1, 0), (1, 1), z_down, mid, FIRST)
    far_up_b = push((1, 0), (1, 3), z_up, mid, FIRST)
    far_down_b = push((1, 0), (1, 1), z_down, 0, mid)
    need(up_b)
    mix(3)
    share((0, 3))
    need(down_b)
    share((0, 1))
    need(far_c)
    share((1, 0))
    for dy in (2, 0):
        back_send(1, dy)
    forward((0, 0), 0, True)
    for rel in [(0, 3), (0, 1), (1, 0)]:
        forward(rel, 0)
    need(down_c)
    mix(2)
    need(up_c)
    share((0, 2))
    for rel in [(0, 2), (0, 1), (0, 3)]:
        back_cross(rel)
    need(shared[0, 0])
    forward((0, 0), 1)
    need(far_up_a)
    far_up_c = push((1, 3), (1, 2), z_up, 0, mid)
    need(far_down_a)
    far_down_c = push((1, 1), (1, 2), z_down, mid, FIRST)

    need(index_near)
    load_index = pltpu.make_async_copy(beside_vmem, beside_index, local_sem.at[len(loads)])
    load_index.start()
    need(near)
    load_index.wait()
    for dy in (1, 3, 2):
        for k in range(SLOTS):
            relayed[dy * SLOTS + k] = beside[beside_index[k, row_of((0, dy))]]
        row_send(1, dy, relayed)
    for rel in [(1, 0), (0, 0)]:
        back_cross(rel)
    for rel in [(1, 2), (1, 1), (1, 3)]:
        back_own(rel)
    ring_start(1, mid, FIRST)
    for dz in (2, 1, 3):
        back_mix(dz)
    need(far_up_b)
    mix_done(3)
    share((1, 3))
    need(far_down_b)
    mix_done(1)
    share((1, 1))
    for rel in [(0, 3), (0, 1), (1, 0)]:
        need(shared[rel])
        forward(rel, 1)
    forward((0, 2), 0)
    need(shared[0, 2])
    forward((0, 2), 1)
    for rel in [(0, 0), (1, 0)]:
        remote_forward(rel)
    for dy in (1, 3, 2):
        need(row_sent[0, dy])
        remote_forward((0, dy))
    for rel in [(1, 3), (1, 1)]:
        forward(rel, 0)
    for rel in [(1, 3), (1, 1)]:
        need(shared[rel])
        forward(rel, 1)
    for dy in (0, 1, 3, 2):
        if dy:
            need(back_sent[1, dy])
        returned_sum(1, dy, beside_index, add_to(beside_sum, dy == 0))
    for b in range(BLOCKS):
        beside_out[b] = beside_sum[b].astype(BF16)
    beside_sent = remote(beside_out, beside_in, x_near)
    need(far_up_c, far_down_c)
    mix_done(2)
    share((1, 2))
    forward((1, 2), 0)
    for dy in (1, 3, 2):
        need(row_sent[1, dy])
        remote_forward((1, dy))
    need(shared[1, 2])
    forward((1, 2), 1)

    for b in range(BLOCKS):
        at = pl.ds(b * TILE, TILE)
        hiddens[at, :] = (inv_col[at, :] * gathered[b]).astype(BF16)
    wg[...] = jnp.dot(cot_t[...], hiddens[...], preferred_element_type=F32)
    half = TILE // 2
    part = half // 8
    mine_half = pl.ds(pl.multiple_of(core * half, half), half)
    other_half = pl.ds(pl.multiple_of((1 - core) * half, half), half)
    halves = remote(wg.at[other_half], wg_core, to_col((0, 0), 1))
    here = x_hi * 4 + z

    def chunk(at):
        return pl.ds(pl.multiple_of(at * part, part), part)

    need(halves)
    wg_part[...] = wg[mine_half, :] + wg_core[...]
    col_parts = []
    for rel in COL_RELS[1:]:
        there = col_of(rel) // 2
        col_parts.append(remote(wg_part.at[chunk(there)], wg_col.at[here], to_col(rel)))
    wg_col[here] = wg_part[chunk(here), :]

    ring_late(1, mid, FIRST)
    for rel in [(0, 2), (0, 1), (0, 3)]:
        back_own(rel)
    for dz in (2, 1, 3):
        back_mix_add(dz)
    ring_start(0, HALF, BLOCKS)
    for dy in (1, 3, 2, 0):
        back_send(0, dy)
    out_z[...] = jnp.dot(hiddens[...], weight[...], preferred_element_type=F32).astype(BF16)
    store_z = pltpu.make_async_copy(out_z, out_z_out, local_sem.at[13])
    store_z.start()
    need(*col_parts)
    wg_mine[...] = jnp.sum(wg_col[...], axis=0)
    row_parts = []
    for rel in ROW_RELS[1:]:
        row_parts.append(remote(wg_mine, wg_row.at[row], to_row(rel)))
    wg_row[row] = wg_mine[...]

    need(*row_parts)
    wg_half[here] = jnp.sum(wg_row[...], axis=0)
    col_full = []
    for rel in COL_RELS[1:]:
        col_full.append(remote(wg_half.at[here], wg_half.at[here], to_col(rel)))

    back_own((1, 0))
    ring_done(1)
    for b in range(BLOCKS):
        value = sums[place((1, 0)), b].astype(F32)
        if b < FIRST:
            value += ring_full[1, 0, b].astype(F32) + ring_full[1, 1, b].astype(F32)
        pair_out[b] = value.astype(BF16)
    pair = remote(pair_out, pair_in, x_far)
    ring_late(0, HALF, BLOCKS)
    back_own((0, 0))
    need(*col_full)
    full = remote(wg_half, wg_other, to_col((0, 0), 1))
    wg_all[mine_half, :] = wg_half[...].reshape(half, TILE)
    need(full)
    wg_all[other_half, :] = wg_other[...].reshape(half, TILE)
    grad_w[...] = wg_all[...].T
    store_w = pltpu.make_async_copy(grad_w, grad_w_out, local_sem.at[14])
    store_w.start()

    for dy in (0, 1, 3, 2):
        if dy:
            need(back_sent[0, dy])
        returned_sum(0, dy, send_index, add_to(spread))
    stores = [store_z, store_w]
    need(beside_sent)
    ring_done(0)
    need(pair)
    for b in range(BLOCKS):
        value = spread[b] + pair_in[b].astype(F32) + beside_in[b].astype(F32)
        value += ring_full[0, 0, b].astype(F32) + ring_full[0, 1, b].astype(F32)
        value *= inv_row[b : b + 1, :]
        grad_x[pl.ds(b * TILE, TILE), :] = value.T.astype(BF16)
        if b % HALF == HALF - 1:
            at = pl.ds((b + 1 - HALF) * TILE, HALF * TILE)
            store = pltpu.make_async_copy(
                grad_x.at[at], grad_x_out.at[at], local_sem.at[15 + b // HALF]
            )
            store.start()
            stores.append(store)
    for copy in copies:
        copy.wait_send()
    for store in stores:
        store.wait()


def on_device(
    features,
    weight,
    cotangent,
    degree,
    tile_vals,
    tile_rows,
    tile_cols,
    tile_live,
    send_index,
    remote_vals,
    remote_rows,
    remote_live,
):
    nodes, width = features.shape
    hbm = pl.BlockSpec(memory_space=pl.ANY)
    stack = (BLOCKS, TILE, TILE)
    n_copies = 96
    return pl.pallas_call(
        kernel,
        out_shape=(
            jax.ShapeDtypeStruct((nodes, width), BF16),
            jax.ShapeDtypeStruct((nodes, width), BF16),
            jax.ShapeDtypeStruct((TILE, TILE), F32),
        ),
        in_specs=[hbm] * 12,
        out_specs=(hbm, hbm, hbm),
        scratch_shapes=[
            pltpu.VMEM((nodes, width), BF16),
            pltpu.VMEM((nodes, width), BF16),
            pltpu.VMEM((TILE, TILE), F32),
            pltpu.VMEM((nodes, width), BF16),
            pltpu.VMEM(weight.shape, BF16),
            pltpu.VMEM((nodes, width), BF16),
            pltpu.VMEM((BLOCKS, TILE), jnp.int32),
        ]
        + [pltpu.SMEM(tile_rows.shape, jnp.int32)] * 3
        + [pltpu.SMEM(send_index.shape[::-1], jnp.int32)] * 3
        + [
            pltpu.VMEM(tile_vals.shape, BF16),
            pltpu.VMEM(remote_vals.shape, BF16),
            pltpu.VMEM((nodes, TILE), F32),
            pltpu.VMEM(stack, BF16),
            pltpu.VMEM((TILE, nodes), BF16),
            pltpu.VMEM((nodes, TILE), BF16),
            pltpu.VMEM((SLOTS, TILE, TILE), F32),
            pltpu.VMEM(stack, F32),
            pltpu.VMEM(stack, F32),
            pltpu.VMEM((32, TILE, TILE), BF16),
            pltpu.VMEM((32, TILE, TILE), BF16),
            pltpu.VMEM((32, TILE, TILE), BF16),
            pltpu.VMEM((32, TILE, TILE), BF16),
            pltpu.VMEM((8,) + stack, BF16),
            pltpu.VMEM((8,) + stack, BF16),
            pltpu.VMEM((8,) + stack, BF16),
            pltpu.VMEM((2,) + stack, BF16),
            pltpu.VMEM((2, 2) + stack, BF16),
            pltpu.VMEM(stack, BF16),
            pltpu.VMEM(stack, BF16),
            pltpu.VMEM((TILE, TILE), F32),
            pltpu.VMEM((TILE // 2, TILE), F32),
            pltpu.VMEM((TILE // 2, TILE), F32),
            pltpu.VMEM((8, 8, TILE), F32),
            pltpu.VMEM((8, TILE), F32),
            pltpu.VMEM((8, 8, TILE), F32),
            pltpu.VMEM((8, 8, TILE), F32),
            pltpu.VMEM((8, 8, TILE), F32),
            pltpu.VMEM((TILE, TILE), F32),
            pltpu.VMEM(stack, BF16),
            pltpu.VMEM(send_index.shape[::-1], jnp.int32),
            pltpu.SMEM(send_index.shape[::-1], jnp.int32),
            pltpu.VMEM((4 * SLOTS, TILE, TILE), BF16),
            pltpu.VMEM(stack, F32),
            pltpu.VMEM(stack, BF16),
            pltpu.VMEM(stack, BF16),
            pltpu.VMEM((3, max(BLOCKS - FIRST, 1), TILE, TILE), BF16),
            pltpu.SemaphoreType.DMA((n_copies,)),
            pltpu.SemaphoreType.DMA((n_copies,)),
            pltpu.SemaphoreType.DMA((17,)),
        ]
        + [pltpu.VMEM(stack, BF16)] * 16,
        compiler_params=pltpu.CompilerParams(
            collective_id=0, has_side_effects=True, vmem_limit_bytes=63 * 2**20
        ),
    )(
        features,
        weight,
        cotangent,
        degree.reshape(BLOCKS, TILE),
        tile_rows,
        tile_cols,
        tile_live,
        send_index.T,
        remote_rows.T,
        remote_live.T,
        tile_vals,
        remote_vals,
    )


def solution(mesh):
    placed = (
        P(("row", "col"), None),
        P(),
        P(("row", "col"), None),
        P(("row", "col")),
        P(("row", "col"), None, None),
        P(("row", "col")),
        P(("row", "col")),
        P(("row", "col")),
        P(("row", "col"), None),
        P(("row", "col"), None, None),
        P(("row", "col"), None),
        P(("row", "col"), None),
    )
    return jax.shard_map(
        on_device,
        mesh=mesh,
        in_specs=placed,
        out_specs=(P(("row", "col"), None), P(("row", "col"), None), P()),
        check_vma=False,
    )
```
